32 devices in a mesh: seg: 8 (over y, x, core), head: 4 (over z).
Axes of the slice: x: 2, y: 2, z: 4, core: 2. Of those that a mesh axis runs over, the one named last changes fastest.
Arguments:
- attn_query: bfloat16 [8, 1024, 3072], P(None, 'seg', 'head'), may hold values from -8 to 8
- attn_key: bfloat16 [8, 1024, 3072], P(None, 'seg', 'head'), may hold values from -8 to 8
- attn_value: bfloat16 [8, 1024, 3072], P(None, 'seg', 'head'), may hold values from -6 to 6
- prompt_len: int32 [8, 8], P(None, 'seg'), may hold values from 1 to 64, as said below
- ttt_weight: bfloat16 [3072, 9216], P(None, 'head'), may hold values from -0.109375 to 0.109375
- init_w1: float32 [48, 64, 256], P('head'), may hold values from -0.75 to 0.75
- init_w2t: float32 [48, 64, 256], P('head'), may hold values from -0.375 to 0.375
- step_rate: float32 [8, 48, 1024], P(None, 'head', 'seg'), may hold values from 0.005 to 0.05
Outputs:
- ttt_out: bfloat16 [8, 1024, 3072], P(None, 'seg', 'head')
The draws below stay inside these ranges and needn't reach their ends.
Inputs may be any that keep to these rules, and one draw needn't show every extreme that they name: `prompt_len`: some entry equals 64.
All inputs are finite; a program needn't handle non-finite values.
Results may differ from the reference program's by a relative error of at most 0.008.
Values may be sent and summed in bfloat16 or wider, within the bound.
No kernel may reach another device: no remote copies, remote signals or barrier semaphores. Data moves between devices by JAX's collectives and lax.ppermute only.
A program may use at most 128 MiB of HBM per device.

```python
import math
import jax
import jax.numpy as jnp
from jax import lax

D = 3072
HEADS = 48
HEAD_DIM = 64
FAST = 256
MINI = 64
TEXT_SLOTS = 64
VIDEOS = 8
SEG_TOK = 128
SEGMENTS = 8
SEQ = 1024


def attention_pair(key):
    key_query, key_key = jax.random.split(jax.random.fold_in(key, 11), 2)
    queries = jnp.clip(jax.random.normal(key_query, (VIDEOS, SEQ, D), jnp.float32), -4.0, 4.0)
    key_rows = jnp.clip(jax.random.normal(key_key, (VIDEOS, SEQ, D), jnp.float32), -4.0, 4.0)
    return (queries, key_rows)


def draw_attn_query(key, part):
    return attention_pair(key)[0].astype(jnp.bfloat16)


def draw_attn_key(key, part):
    return attention_pair(key)[1].astype(jnp.bfloat16)


def draw_prompt_len(key, part):
    key_lengths, key_place = jax.random.split(jax.random.fold_in(key, 23))
    lengths = jax.random.randint(key_lengths, (VIDEOS * SEGMENTS,), 1, TEXT_SLOTS + 1)
    place = jax.random.randint(key_place, (), 0, VIDEOS * SEGMENTS)
    lengths = lengths.at[place].set(TEXT_SLOTS)
    return lengths.reshape(VIDEOS, SEGMENTS).astype(jnp.int32)


def level_of(rng, dims, cuts, low, high):
    gain = 1.0
    for axis_at, shards_of in cuts:
        draws = jax.random.uniform(jax.random.fold_in(jax.random.fold_in(rng, 6), axis_at), (shards_of,), jnp.float32, low / len(cuts), high / len(cuts))
        gain = gain * jnp.repeat(jnp.exp(draws), dims[axis_at] // shards_of).reshape((-1,) + (1,) * (len(dims) - 1 - axis_at))
    return gain


def centred(key, extent, deviation, limit, cuts=(), kind=jnp.bfloat16):
    entries = deviation * jax.random.normal(key, extent, jnp.float32)
    if cuts:
        entries = entries * level_of(key, extent, cuts, -0.22, 0.18)
    return jnp.clip(entries, -limit, limit).astype(kind)


def setup_inputs(seed: int = 0) -> dict:
    key_of = jax.random.split(jax.random.key(seed), 9)
    return {
        "attn_query": draw_attn_query(jax.random.fold_in(key_of[8], 71), 0),
        "attn_key": draw_attn_key(jax.random.fold_in(key_of[8], 71), 0),
        "attn_value": centred(key_of[2], (VIDEOS, SEQ, D), 1.0, 6.0, ((1, 8), (2, 4))),
        "prompt_len": draw_prompt_len(jax.random.fold_in(key_of[8], 71), 0),
        "ttt_weight": centred(key_of[4], (D, 3 * D), D ** -0.5, 0.109375, ((1, 4),)),
        "init_w1": centred(key_of[5], (HEADS, HEAD_DIM, FAST), HEAD_DIM ** -0.5, 0.75, ((0, 4),), jnp.float32),
        "init_w2t": centred(key_of[6], (HEADS, HEAD_DIM, FAST), FAST ** -0.5, 0.375, ((0, 4),), jnp.float32),
        "step_rate": jnp.clip(jnp.exp(math.log(0.05) - 2.3025851 * jax.random.uniform(key_of[7], (VIDEOS, HEADS, SEQ), jnp.float32) ** level_of(key_of[7], (VIDEOS, HEADS, SEQ), ((1, 4), (2, 8)), -0.2, 0.2)), 0.005, 0.05),
    }


highest_precision = lax.Precision.HIGHEST
norm_epsilon = 1e-05
rms_epsilon = 1e-06

def normalize(values):
    center = values - lax.optimization_barrier(jnp.mean(values, axis=-1, keepdims=True))
    spread = lax.optimization_barrier(jnp.mean(center * center, axis=-1, keepdims=True))
    return center * lax.rsqrt(spread + norm_epsilon)

def fast_mlp(inputs, fast_weights):
    hidden = jax.nn.gelu(jnp.einsum('bmd,bdf->bmf', inputs, fast_weights[:, 0], precision=highest_precision), approximate=True)
    return normalize(jnp.einsum('bmf,bdf->bmd', hidden, fast_weights[:, 1], precision=highest_precision))

def minibatch(fast_weights, batch_items):
    queries, key_rows, value_rows, step_rates = batch_items
    target = value_rows - key_rows

    def loss_value(weights_now):
        error = fast_mlp(key_rows, weights_now) - target
        return 0.5 * jnp.sum(step_rates[:, :, None] * error * error) / step_rates.shape[-1]
    gradient = jax.grad(loss_value)(fast_weights)
    fast_weights = fast_weights - gradient
    return (fast_weights, queries + fast_mlp(queries, fast_weights))

def segment_attention(operands):
    query_block, key_block, value_block, length = operands
    position = jnp.arange(SEG_TOK, dtype=jnp.int32)
    usable = (position >= TEXT_SLOTS) | (position < length)
    scores = jnp.einsum('qhd,khd->hqk', query_block.astype(jnp.float32), key_block.astype(jnp.float32)) * HEAD_DIM ** (-0.5)
    scores = jnp.where(usable[None, None, :], scores, -1e+30)
    largest = lax.optimization_barrier(jnp.max(scores, axis=-1, keepdims=True))
    exponent = jnp.exp(scores - largest)
    weights = (exponent / lax.optimization_barrier(jnp.sum(exponent, axis=-1, keepdims=True))).astype(jnp.bfloat16)
    mixed = jnp.einsum('hqk,khd->qhd', weights.astype(jnp.float32), value_block.astype(jnp.float32))
    return mixed.astype(jnp.bfloat16)

def reference(attn_query, attn_key, attn_value, prompt_len, ttt_weight, init_w1, init_w2t, step_rate):
    block_count = VIDEOS * SEGMENTS

    def reshape_blocks(array):
        return array.reshape(block_count, SEG_TOK, HEADS, HEAD_DIM)
    attended = lax.map(segment_attention, (reshape_blocks(attn_query), reshape_blocks(attn_key), reshape_blocks(attn_value), prompt_len.reshape(block_count)))
    features = attended.reshape(VIDEOS * SEQ, D).astype(jnp.float32)
    normed = (features * lax.rsqrt(lax.optimization_barrier(jnp.mean(features * features, axis=-1, keepdims=True)) + rms_epsilon)).astype(jnp.bfloat16)
    projected = jnp.dot(normed, ttt_weight, preferred_element_type=jnp.float32)
    projected = projected.reshape(VIDEOS, SEQ, HEADS, 3, HEAD_DIM).transpose(0, 2, 3, 1, 4)
    step_count = SEQ // MINI

    def to_blocks(array):
        return array.reshape(VIDEOS * HEADS, step_count, MINI, HEAD_DIM).transpose(1, 0, 2, 3)
    position = jnp.arange(SEQ, dtype=jnp.int32)
    within = position % SEG_TOK
    segment = position // SEG_TOK
    lengths = prompt_len[:, segment]
    usable = (within >= TEXT_SLOTS)[None, :] | (within[None, :] < lengths)
    step_rates = step_rate * usable[:, None, :].astype(jnp.float32)
    rate_blocks = step_rates.reshape(VIDEOS * HEADS, step_count, MINI).transpose(1, 0, 2)
    start = jnp.stack([init_w1, init_w2t], axis=1)
    start = jnp.broadcast_to(start[None], (VIDEOS,) + start.shape).reshape(VIDEOS * HEADS, 2, HEAD_DIM, FAST)
    final_weights, outputs = lax.scan(minibatch, start, (to_blocks(projected[:, :, 0]), to_blocks(projected[:, :, 1]), to_blocks(projected[:, :, 2]), rate_blocks))
    outputs = outputs.transpose(1, 0, 2, 3).reshape(VIDEOS, HEADS, SEQ, HEAD_DIM).transpose(0, 2, 1, 3)
    return outputs.reshape(VIDEOS, SEQ, D).astype(jnp.bfloat16)
```

```python
import functools
import jax
import jax.numpy as jnp
from jax import lax
from jax.experimental import pallas as pl
from jax.experimental.pallas import tpu as pltpu
from jax.sharding import PartitionSpec as P

highest_precision = lax.Precision.HIGHEST
MINI = 64
TEXT_SLOTS = 64
norm_epsilon = 1e-05
rms_epsilon = 1e-06
VMEM_LIMIT = 56 * 1024 * 1024
gelu_a = 0.7978845608028654
gelu_b = gelu_a * 0.044715


def dot_nn(a, b):
    return lax.dot_general(a, b, (((1,), (0,)), ((), ())), preferred_element_type=jnp.float32)


def dot_nt(a, b):
    return lax.dot_general(a, b, (((1,), (1,)), ((), ())), preferred_element_type=jnp.float32)


def low_half(shape, half):
    return lax.broadcasted_iota(jnp.int32, shape, len(shape) - 1) < half


def half_ones(half):
    width = 2 * half
    row = lax.broadcasted_iota(jnp.int32, (width, width), 0) < half
    column = lax.broadcasted_iota(jnp.int32, (width, width), 1) < half
    return (row == column).astype(jnp.bfloat16)


def attention_kernel(lens_ref, q_ref, k_ref, v_ref, rate_ref, out_ref, *, half):
    video = pl.program_id(0)
    length = lens_ref[video]
    seg_len = q_ref.shape[1]
    channels = q_ref.shape[2]
    width = 2 * half
    heads = channels // half
    key_at = lax.broadcasted_iota(jnp.int32, (seg_len, 2 * seg_len), 1)
    key_at = jnp.where(key_at >= seg_len, key_at - seg_len, key_at)
    usable = (key_at >= TEXT_SLOTS) | (key_at < length)
    low = low_half((seg_len, width), half)
    zero = jnp.zeros((seg_len, width), jnp.bfloat16)
    ones = jnp.ones((seg_len, width), jnp.bfloat16)
    scale = jnp.asarray(half ** (-0.5), jnp.bfloat16)
    totals = jnp.concatenate([jnp.where(low, ones, zero), jnp.where(low, zero, ones)], axis=0)
    for pair in range(channels // width):
        lanes = slice(pair * width, (pair + 1) * width)
        query = q_ref[0, :, lanes] * scale
        key = k_ref[0, :, lanes]
        value = v_ref[0, :, lanes]
        keys = jnp.concatenate([jnp.where(low, key, zero), jnp.where(low, zero, key)], axis=0)
        scores = jnp.where(usable, dot_nt(query, keys), -1e30)
        parts = []
        for side in range(2):
            block = scores[:, side * seg_len : (side + 1) * seg_len]
            largest = jnp.max(block, axis=1, keepdims=True)
            parts.append(jnp.exp(block - largest).astype(jnp.bfloat16))
        weights = jnp.concatenate(parts, axis=1)
        values = jnp.concatenate([jnp.where(low, value, zero), jnp.where(low, zero, value)], axis=0)
        mixed = dot_nn(weights, jnp.concatenate([values, totals], axis=1))
        out_ref[0, :, lanes] = (mixed[:, :width] / mixed[:, width:]).astype(jnp.bfloat16)
    token = lax.broadcasted_iota(jnp.int32, (seg_len, 1), 0)
    open_token = ((token >= TEXT_SLOTS) | (token < length)).astype(jnp.float32)
    rates = rate_ref[0]
    spare = out_ref.shape[2] - channels
    rates = jnp.concatenate(
        [rates, jnp.zeros((spare - rates.shape[0], seg_len), jnp.float32)], axis=0
    )
    out_ref[0, :, channels:] = (rates.T * open_token).astype(jnp.bfloat16)


def attention(attn_query, attn_key, attn_value, lens, step_rate, half):
    videos, seg_len, channels = attn_query.shape
    heads = step_rate.shape[1]
    spare = 128
    block = pl.BlockSpec((1, seg_len, channels), lambda v, lens: (v, 0, 0))
    return pl.pallas_call(
        functools.partial(attention_kernel, half=half),
        grid_spec=pltpu.PrefetchScalarGridSpec(
            num_scalar_prefetch=1,
            grid=(videos,),
            in_specs=[block, block, block, pl.BlockSpec((1, heads, seg_len), lambda v, lens: (v, 0, 0))],
            out_specs=pl.BlockSpec((1, seg_len, channels + spare), lambda v, lens: (v, 0, 0)),
        ),
        out_shape=jax.ShapeDtypeStruct((videos, seg_len, channels + spare), jnp.bfloat16),
        compiler_params=pltpu.CompilerParams(vmem_limit_bytes=VMEM_LIMIT),
        name="attention",
    )(lens, attn_query, attn_key, attn_value, step_rate)


def project_kernel(row_ref, *refs, shards, half):
    x_refs = refs[:shards]
    rate_ref, w_ref, q_ref, k_ref, t_ref, e_ref, inv_ref = refs[shards:]
    pair = pl.program_id(0)
    tokens, depth = x_refs[0].shape
    width = 2 * half

    @pl.when(pair == 0)
    def _():
        total = jnp.zeros((tokens, 128), jnp.float32)
        for x_ref in x_refs:
            for at in range(0, depth, 128):
                piece = x_ref[:, at : at + 128].astype(jnp.float32)
                total = total + piece * piece
        mean = jnp.sum(total, axis=1, keepdims=True) / (shards * depth)
        inv_ref[...] = jnp.broadcast_to(lax.rsqrt(mean + rms_epsilon), inv_ref.shape)

    acc = None
    for i, x_ref in enumerate(x_refs):
        rows = pl.ds(pl.multiple_of(row_ref[i] * depth, depth), depth)
        term = dot_nn(x_ref[...], w_ref[rows, :])
        acc = term if acc is None else acc + term
    inv = inv_ref[...]
    low = low_half((tokens, width), half)
    first = acc[:, :width] * inv
    middle = acc[:, width : 2 * width] * inv
    last = acc[:, 2 * width :] * inv
    query = jnp.where(low, first, middle)
    key = pltpu.roll(jnp.where(low, last, first), half, 1)
    target = jnp.where(low, middle, last) - key
    zero = jnp.zeros_like(target)
    total_low = jnp.sum(jnp.where(low, target, zero), axis=1, keepdims=True)
    total_high = jnp.sum(jnp.where(low, zero, target), axis=1, keepdims=True)
    target = target - jnp.where(low, total_low, total_high) * (1.0 / half)
    q_ref[...] = query
    k_ref[...] = key.astype(jnp.bfloat16)
    t_ref[...] = target
    head = lax.broadcasted_iota(jnp.int32, (rate_ref.shape[1], width), 0)
    lane = lax.broadcasted_iota(jnp.int32, (rate_ref.shape[1], width), 1)
    spread = (head == 2 * pair + (lane >= half).astype(jnp.int32)).astype(jnp.bfloat16)
    e_ref[...] = dot_nn(rate_ref[...], spread) * (1.0 / MINI)


def project(shards, rates, weight, row_blocks, half):
    tokens, depth = shards[0].shape
    width = 2 * half
    pairs = weight.shape[1] // (3 * width)
    whole = pl.BlockSpec((tokens, depth), lambda p, r: (0, 0))
    piece = pl.BlockSpec((tokens, width), lambda p, r: (0, p))
    out = lambda kind: jax.ShapeDtypeStruct((tokens, pairs * width), kind)
    return pl.pallas_call(
        functools.partial(project_kernel, shards=len(shards), half=half),
        grid_spec=pltpu.PrefetchScalarGridSpec(
            num_scalar_prefetch=1,
            grid=(pairs,),
            in_specs=[whole] * len(shards)
            + [
                pl.BlockSpec(rates.shape, lambda p, r: (0, 0)),
                pl.BlockSpec((weight.shape[0], 3 * width), lambda p, r: (0, p)),
            ],
            out_specs=[piece] * 4,
            scratch_shapes=[pltpu.VMEM((tokens, width), jnp.float32)],
        ),
        out_shape=[out(jnp.float32), out(jnp.bfloat16), out(jnp.float32), out(jnp.float32)],
        compiler_params=pltpu.CompilerParams(vmem_limit_bytes=VMEM_LIMIT),
        name="project",
    )(row_blocks, *shards, rates, weight)


def ttt_kernel(q_ref, k_ref, t_ref, e_ref, w1_in, w2_in, out_ref, w1_out, w2_out, w1_s, w2_s, *, half):
    width = 2 * half
    steps = q_ref.shape[0] // MINI
    pairs = q_ref.shape[1] // width
    hidden = w1_in.shape[2]
    block_ones = half_ones(half)

    w1_out[...] = w1_in[...]
    w2_out[...] = w2_in[...]
    for head in range(2 * pairs):
        here = slice((head % 2) * half, (head % 2) * half + half)
        other = slice(half - (head % 2) * half, 2 * half - (head % 2) * half)
        w1_s[head, here, :] = w1_in[head].astype(jnp.bfloat16)
        w1_s[head, other, :] = jnp.zeros((half, hidden), jnp.bfloat16)
        w2_s[head, here, :] = w2_in[head].astype(jnp.bfloat16)
        w2_s[head, other, :] = jnp.zeros((half, hidden), jnp.bfloat16)

    def rows_of(step):
        return pl.ds(pl.multiple_of(step * MINI, MINI), MINI)

    def gelu_parts(value):
        square = value * value
        return square, jnp.tanh(value * (gelu_b * square + gelu_a))

    def forward(pair, batch, grads):
        hiddens, slopes = [], []
        total = None
        for side in range(2):
            head = 2 * pair + side
            value = dot_nn(batch, w1_s[head])
            square, bent = gelu_parts(value)
            doubled = (value + value * bent).astype(jnp.bfloat16)
            if grads:
                v, s, b = value[-MINI:], square[-MINI:], bent[-MINI:]
                slopes.append((1.0 + b) + v * (1.0 - b * b) * (3.0 * gelu_b * s + gelu_a))
                hiddens.append(doubled[-MINI:])
            term = dot_nt(doubled, w2_s[head])
            total = term if total is None else total + term
        spread = dot_nn((total * total).astype(jnp.bfloat16), block_ones)
        inverse = lax.rsqrt(spread * (1.0 / half) + 4.0 * norm_epsilon)
        return total * inverse, inverse, hiddens, slopes

    def update(pair, step, unit, inverse, hiddens, slopes):
        lanes = slice(pair * width, (pair + 1) * width)
        rows = rows_of(step)
        grad = e_ref[rows, lanes] * (unit - t_ref[rows, lanes])
        along = dot_nn((grad * unit).astype(jnp.bfloat16), block_ones) * (1.0 / half)
        change = (inverse * (grad - unit * along)).astype(jnp.bfloat16)
        change_t = change.T
        key_t = k_ref[rows, lanes].T
        for side in range(2):
            head = 2 * pair + side
            here = slice(side * half, side * half + half)
            back = (dot_nn(change, w2_s[head]) * slopes[side]).astype(jnp.bfloat16)
            w2 = w2_out[head] - dot_nn(change_t[here], hiddens[side])
            w2_out[head] = w2
            w1 = w1_out[head] - dot_nn(key_t[here], back)
            w1_out[head] = w1
            w2_s[head, here, :] = w2.astype(jnp.bfloat16)
            w1_s[head, here, :] = w1.astype(jnp.bfloat16)

    def one(step, with_query, with_key):
        for pair in range(pairs):
            lanes = slice(pair * width, (pair + 1) * width)
            parts = []
            if with_query:
                query = q_ref[rows_of(step - 1), lanes]
                parts.append(query.astype(jnp.bfloat16))
            if with_key:
                parts.append(k_ref[rows_of(step), lanes])
            batch = jnp.concatenate(parts, axis=0) if len(parts) > 1 else parts[0]
            unit, inverse, hiddens, slopes = forward(pair, batch, with_key)
            if with_query:
                out_ref[rows_of(step - 1), lanes] = (query + unit[:MINI]).astype(jnp.bfloat16)
            if with_key:
                update(pair, step, unit[-MINI:], inverse[-MINI:], hiddens, slopes)

    one(0, False, True)
    lax.fori_loop(1, steps, lambda step, carry: (one(step, True, True), carry)[1], 0)
    one(steps, True, False)


def ttt(query, key, target, rates, w1, w2, half):
    hidden = w1.shape[2]
    heads = w1.shape[0]
    state = jax.ShapeDtypeStruct(w1.shape, jnp.float32)
    return pl.pallas_call(
        functools.partial(ttt_kernel, half=half),
        out_shape=[jax.ShapeDtypeStruct(query.shape, jnp.bfloat16), state, state],
        scratch_shapes=[pltpu.VMEM((heads, 2 * half, hidden), jnp.bfloat16)] * 2,
        compiler_params=pltpu.CompilerParams(vmem_limit_bytes=VMEM_LIMIT),
        name="fast_weights",
    )(query, key, target, rates, w1, w2)


def normalize(values):
    center = values - jnp.mean(values, axis=-1, keepdims=True)
    spread = jnp.mean(center * center, axis=-1, keepdims=True)
    return center * lax.rsqrt(spread + norm_epsilon)


def fast_mlp(inputs, fast_weights):
    hidden = jax.nn.gelu(
        jnp.einsum("bmd,bdf->bmf", inputs, fast_weights[:, 0], precision=highest_precision),
        approximate=True,
    )
    return normalize(
        jnp.einsum("bmf,bdf->bmd", hidden, fast_weights[:, 1], precision=highest_precision)
    )


def minibatch(fast_weights, batch_items):
    queries, key_rows, value_rows, step_rates = batch_items
    target = value_rows - key_rows

    def loss_value(weights_now):
        error = fast_mlp(key_rows, weights_now) - target
        return 0.5 * jnp.sum(step_rates[:, :, None] * error * error) / step_rates.shape[-1]

    gradient = jax.grad(loss_value)(fast_weights)
    fast_weights = fast_weights - gradient
    return (fast_weights, queries + fast_mlp(queries, fast_weights))


def run_items(fast_weights, picked, step_rates):
    batch = picked.shape[0]
    seg_len = picked.shape[2]
    head_dim = picked.shape[3]
    block_count = seg_len // MINI

    def to_blocks(array):
        return array.reshape(batch, block_count, MINI, head_dim).transpose(1, 0, 2, 3)

    rate_blocks = step_rates.reshape(batch, block_count, MINI).transpose(1, 0, 2)
    fast_weights, outputs = lax.scan(
        minibatch,
        fast_weights,
        (to_blocks(picked[:, 0]), to_blocks(picked[:, 1]), to_blocks(picked[:, 2]), rate_blocks),
    )
    return (fast_weights, outputs.transpose(1, 0, 2, 3).reshape(batch, seg_len, head_dim))


def any_size(attn_query, attn_key, attn_value, prompt_len, ttt_weight, init_w1, init_w2t, step_rate):
    videos = attn_query.shape[0]
    seg_len = attn_query.shape[1]
    heads_dev = init_w1.shape[0]
    head_dim = init_w1.shape[1]
    position = lax.broadcasted_iota(jnp.int32, (videos, seg_len), 1)
    usable = (position >= TEXT_SLOTS) | (position < prompt_len)
    queries = attn_query.reshape(videos, seg_len, heads_dev, head_dim)
    key_rows = attn_key.reshape(videos, seg_len, heads_dev, head_dim)
    value_rows = attn_value.reshape(videos, seg_len, heads_dev, head_dim)
    scores = jnp.einsum(
        "vqhd,vkhd->vhqk", queries, key_rows, preferred_element_type=jnp.float32
    ) * head_dim ** (-0.5)
    scores = jnp.where(usable[:, None, None, :], scores, -1e30)
    largest = jnp.max(scores, axis=-1, keepdims=True)
    exponent = jnp.exp(scores - largest)
    weights = (exponent / jnp.sum(exponent, axis=-1, keepdims=True)).astype(jnp.bfloat16)
    attended = jnp.einsum(
        "vhqk,vkhd->vqhd", weights, value_rows, preferred_element_type=jnp.float32
    )
    attended = attended.astype(jnp.bfloat16).reshape(videos, seg_len, heads_dev * head_dim)
    features = lax.all_gather(attended, "head", axis=2, tiled=True)
    feature_full = features.astype(jnp.float32)
    normed = (
        feature_full
        * lax.rsqrt(jnp.mean(feature_full * feature_full, axis=-1, keepdims=True) + rms_epsilon)
    ).astype(jnp.bfloat16)
    projected = jnp.dot(
        normed.reshape(videos * seg_len, normed.shape[2]),
        ttt_weight,
        preferred_element_type=jnp.float32,
    )
    projected = projected.reshape(videos, seg_len, heads_dev, 3, head_dim).transpose(0, 2, 3, 1, 4)
    step_rates = step_rate * usable[:, None, :].astype(jnp.float32)
    init_stack = jnp.stack([init_w1, init_w2t], axis=1)
    seg_count = lax.axis_size("seg")
    item_count = videos * heads_dev
    per_device = (item_count + seg_count - 1) // seg_count
    padded = per_device * seg_count
    item_inputs = projected.reshape(item_count, 3, seg_len, head_dim)
    item_inputs = jnp.pad(item_inputs, ((0, padded - item_count), (0, 0), (0, 0), (0, 0)))
    item_rates = step_rates.reshape(item_count, 1, seg_len, 1)
    item_rates = jnp.pad(item_rates, ((0, padded - item_count), (0, 0), (0, 0), (0, 0)))
    sequences, rate_rows = (
        lax.all_to_all(
            item_inputs.astype(jnp.bfloat16), "seg", split_axis=0, concat_axis=2, tiled=True
        ).astype(item_inputs.dtype),
        lax.all_to_all(
            item_rates.astype(jnp.bfloat16), "seg", split_axis=0, concat_axis=2, tiled=True
        ).astype(item_rates.dtype),
    )
    item_global = lax.axis_index("seg") * per_device + jnp.arange(per_device, dtype=jnp.int32)
    head_of = item_global % heads_dev
    start = jnp.take(init_stack, head_of, axis=0)
    final_weights, outputs = run_items(
        start, sequences, rate_rows.reshape(per_device, sequences.shape[2])
    )
    returned = lax.all_to_all(
        outputs.astype(jnp.bfloat16), "seg", split_axis=1, concat_axis=0, tiled=True
    ).astype(outputs.dtype)
    results = returned[:item_count].reshape(videos, heads_dev, seg_len, head_dim)
    results = results.transpose(0, 2, 1, 3).reshape(videos, seg_len, heads_dev * head_dim)
    return results.astype(jnp.bfloat16)


def gather_heads(block):
    count = lax.axis_size("head")
    me = lax.axis_index("head")
    if count != 4:
        every = lax.all_gather(block, "head", axis=0)
        return [every[i] for i in range(count)], jnp.arange(count, dtype=jnp.int32)
    near = lax.ppermute(block, "head", [(0, 1), (1, 0), (2, 3), (3, 2)])
    far = lax.ppermute(block, "head", [(0, 2), (2, 0), (1, 3), (3, 1)])
    inner = lax.ppermute(block, "head", [(1, 2), (2, 1)])
    outer = lax.ppermute(far, "head", [(2, 3), (1, 0)])
    last = jnp.where((me == 0) | (me == 3), outer, inner)
    return [block, near, far, last], me ^ jnp.arange(4, dtype=jnp.int32)


def by_video(attn_query, attn_key, attn_value, prompt_len, ttt_weight, init_w1, init_w2t, step_rate):
    videos, seg_len, channels = attn_query.shape
    half = init_w1.shape[1]
    segments = lax.axis_size("seg")
    mixed = attention(attn_query, attn_key, attn_value, prompt_len[:, 0], step_rate, half)
    mine = lax.all_to_all(mixed, "seg", split_axis=0, concat_axis=0, tiled=True)
    mine = mine.reshape(segments * seg_len, mixed.shape[2])
    features = mine[:, :channels]
    rates = mine[:, channels:]
    w1 = init_w1
    w2 = init_w2t - jnp.mean(init_w2t, axis=1, keepdims=True)
    tokens = segments * seg_len
    chunk = max(seg_len, tokens // 4)
    outs = []
    for at in range(0, tokens, chunk):
        shards, row_blocks = gather_heads(features[at : at + chunk])
        query, key, target, spread = project(shards, rates[at : at + chunk], ttt_weight, row_blocks, half)
        out, w1, w2 = ttt(query, key, target, spread, w1, w2, half)
        outs.append(out)
    result = jnp.concatenate(outs, axis=0).reshape(videos, seg_len, channels)
    return lax.all_to_all(result, "seg", split_axis=0, concat_axis=0, tiled=True)


def body(attn_query, attn_key, attn_value, prompt_len, ttt_weight, init_w1, init_w2t, step_rate):
    videos, seg_len, channels = attn_query.shape
    heads, half, hidden = init_w1.shape
    whole_pairs = heads % 2 == 0 and 2 * half == 128 and hidden % 128 == 0
    fits = seg_len % 128 == 0 and heads <= 128
    run = by_video if videos == lax.axis_size("seg") and whole_pairs and fits else any_size
    return run(attn_query, attn_key, attn_value, prompt_len, ttt_weight, init_w1, init_w2t, step_rate)


def solution(mesh):
    return jax.shard_map(
        body,
        mesh=mesh,
        in_specs=(
            P(None, "seg", "head"),
            P(None, "seg", "head"),
            P(None, "seg", "head"),
            P(None, "seg"),
            P(None, "head"),
            P("head", None, None),
            P("head", None, None),
            P(None, "head", "seg"),
        ),
        out_specs=P(None, "seg", "head"),
        check_vma=False,
    )
```

```python
import functools
import jax
import jax.numpy as jnp
from jax import lax
from jax.experimental import pallas as pl
from jax.experimental.pallas import tpu as pltpu
from jax.sharding import PartitionSpec as P

highest_precision = lax.Precision.HIGHEST
MINI = 64
TEXT_SLOTS = 64
norm_epsilon = 1e-05
rms_epsilon = 1e-06
GROUP = 6
PB = 3
CHUNK_VMEM = 26 * 1024 * 1024
VMEM_LIMIT = 20 * 1024 * 1024
gelu_a = 0.7978845608028654
gelu_b = gelu_a * 0.044715


def dot_nn(a, b):
    return lax.dot_general(a, b, (((1,), (0,)), ((), ())), preferred_element_type=jnp.float32)


def dot_nt(a, b):
    return lax.dot_general(a, b, (((1,), (1,)), ((), ())), preferred_element_type=jnp.float32)


def low_half(shape, half):
    return lax.broadcasted_iota(jnp.int32, shape, len(shape) - 1) < half


def half_ones(half):
    width = 2 * half
    row = lax.broadcasted_iota(jnp.int32, (width, width), 0) < half
    column = lax.broadcasted_iota(jnp.int32, (width, width), 1) < half
    return (row == column).astype(jnp.bfloat16)


def attention_kernel(lens_ref, q_ref, k_ref, v_ref, rate_ref, out_ref, *, half):
    video = pl.program_id(0)
    length = lens_ref[video]
    seg_len = q_ref.shape[1]
    channels = q_ref.shape[2]
    width = 2 * half
    heads = channels // half
    key_at = lax.broadcasted_iota(jnp.int32, (seg_len, 2 * seg_len), 1)
    key_at = jnp.where(key_at >= seg_len, key_at - seg_len, key_at)
    usable = (key_at >= TEXT_SLOTS) | (key_at < length)
    low = low_half((seg_len, width), half)
    zero = jnp.zeros((seg_len, width), jnp.bfloat16)
    ones = jnp.ones((seg_len, width), jnp.bfloat16)
    scale = jnp.asarray(half ** (-0.5), jnp.bfloat16)
    totals = jnp.concatenate([jnp.where(low, ones, zero), jnp.where(low, zero, ones)], axis=0)
    for pair in range(channels // width):
        lanes = slice(pair * width, (pair + 1) * width)
        query = q_ref[0, :, lanes] * scale
        key = k_ref[0, :, lanes]
        value = v_ref[0, :, lanes]
        keys = jnp.concatenate([jnp.where(low, key, zero), jnp.where(low, zero, key)], axis=0)
        scores = jnp.where(usable, dot_nt(query, keys), -1e30)
        parts = []
        for side in range(2):
            block = scores[:, side * seg_len : (side + 1) * seg_len]
            largest = jnp.max(block, axis=1, keepdims=True)
            parts.append(jnp.exp(block - largest).astype(jnp.bfloat16))
        weights = jnp.concatenate(parts, axis=1)
        values = jnp.concatenate([jnp.where(low, value, zero), jnp.where(low, zero, value)], axis=0)
        mixed = dot_nn(weights, jnp.concatenate([values, totals], axis=1))
        out_ref[0, :, lanes] = (mixed[:, :width] / mixed[:, width:]).astype(jnp.bfloat16)
    token = lax.broadcasted_iota(jnp.int32, (seg_len, 1), 0)
    open_token = ((token >= TEXT_SLOTS) | (token < length)).astype(jnp.float32)
    rates = rate_ref[0]
    spare = out_ref.shape[2] - channels
    rates = jnp.concatenate(
        [rates, jnp.zeros((spare - rates.shape[0], seg_len), jnp.float32)], axis=0
    )
    out_ref[0, :, channels:] = (rates.T * open_token).astype(jnp.bfloat16)


def attention(attn_query, attn_key, attn_value, lens, step_rate, half):
    videos, seg_len, channels = attn_query.shape
    heads = step_rate.shape[1]
    spare = 128
    block = pl.BlockSpec((1, seg_len, channels), lambda v, lens: (v, 0, 0))
    return pl.pallas_call(
        functools.partial(attention_kernel, half=half),
        grid_spec=pltpu.PrefetchScalarGridSpec(
            num_scalar_prefetch=1,
            grid=(videos,),
            in_specs=[block, block, block, pl.BlockSpec((1, heads, seg_len), lambda v, lens: (v, 0, 0))],
            out_specs=pl.BlockSpec((1, seg_len, channels + spare), lambda v, lens: (v, 0, 0)),
        ),
        out_shape=jax.ShapeDtypeStruct((videos, seg_len, channels + spare), jnp.bfloat16),
        compiler_params=pltpu.CompilerParams(vmem_limit_bytes=VMEM_LIMIT),
        name="attention",
    )(lens, attn_query, attn_key, attn_value, step_rate)


def chunk_kernel(row_ref, *refs, inputs, shards, half, extra):
    x_refs, refs = refs[:inputs], refs[inputs:]
    rate_ref, w_ref, w1_in, w2_in = refs[:4]
    out_ref, w1_out, w2_out = refs[4 + extra : 7 + extra]
    x_s, q_ref, k_ref, t_ref, e_ref, w1_s, w2_s = refs[7 + extra :]
    tokens, depth = x_refs[0].shape
    width = 2 * half
    steps = tokens // MINI
    pairs = q_ref.shape[1] // width
    hidden = w1_in.shape[2]
    block_ones = half_ones(half)

    w1_out[...] = w1_in[...]
    w2_out[...] = w2_in[...]
    for head in range(2 * pairs):
        here = slice((head % 2) * half, (head % 2) * half + half)
        other = slice(half - (head % 2) * half, 2 * half - (head % 2) * half)
        w1_s[head, here, :] = w1_in[head].astype(jnp.bfloat16)
        w1_s[head, other, :] = jnp.zeros((half, hidden), jnp.bfloat16)
        w2_s[head, here, :] = w2_in[head].astype(jnp.bfloat16)
        w2_s[head, other, :] = jnp.zeros((half, hidden), jnp.bfloat16)

    squares = jnp.zeros((tokens, 128), jnp.float32)
    for i in range(shards):
        start = row_ref[i] * depth
        for at in range(0, depth, 128):
            piece = x_refs[i][:, at : at + 128]
            if i == shards - 1 and inputs > shards:
                piece = piece + x_refs[shards][:, at : at + 128]
            x_s[:, pl.ds(pl.multiple_of(start + at, 128), 128)] = piece
            wide = piece.astype(jnp.float32)
            squares = squares + wide * wide
    mean = jnp.sum(squares, axis=1, keepdims=True) / (shards * depth)
    inv = jnp.broadcast_to(lax.rsqrt(mean + rms_epsilon), (tokens, width))

    low = low_half((tokens, width), half)
    zero = jnp.zeros((tokens, width), jnp.float32)
    block = PB if pairs % PB == 0 else 1
    for group in range(0, pairs, block):
        wide = 3 * width * block
        acc = dot_nn(x_s[...], w_ref[:, group * 3 * width : group * 3 * width + wide])
        for at in range(block):
            first, middle, last = (
                acc[:, (3 * at + j) * width : (3 * at + j + 1) * width] * inv for j in range(3)
            )
            query = jnp.where(low, first, middle)
            key = pltpu.roll(jnp.where(low, last, first), half, 1)
            target = jnp.where(low, middle, last) - key
            total_low = jnp.sum(jnp.where(low, target, zero), axis=1, keepdims=True)
            total_high = jnp.sum(jnp.where(low, zero, target), axis=1, keepdims=True)
            target = target - jnp.where(low, total_low, total_high) * (1.0 / half)
            lanes = slice((group + at) * width, (group + at + 1) * width)
            q_ref[:, lanes] = query
            k_ref[:, lanes] = key.astype(jnp.bfloat16)
            t_ref[:, lanes] = target
    head = lax.broadcasted_iota(jnp.int32, (rate_ref.shape[1], pairs * width), 0)
    lane = lax.broadcasted_iota(jnp.int32, (rate_ref.shape[1], pairs * width), 1)
    spread_to = (lane // half == head).astype(jnp.bfloat16)
    e_ref[...] = dot_nn(rate_ref[...], spread_to) * (1.0 / MINI)

    def rows_of(step):
        return pl.ds(pl.multiple_of(step * MINI, MINI), MINI)

    def gelu_parts(value):
        square = value * value
        return square, jnp.tanh(value * (gelu_b * square + gelu_a))

    def one(step, with_query, with_key):
        for first in range(0, pairs, GROUP):
            group = range(first, min(first + GROUP, pairs))
            sides = [(pair, side) for pair in group for side in range(2)]
            lanes = {pair: slice(pair * width, (pair + 1) * width) for pair in group}
            batch, value, doubled, slope, total, inverse, unit, change = ({} for _ in range(8))
            for pair in group:
                parts = []
                if with_query:
                    parts.append(q_ref[rows_of(step - 1), lanes[pair]].astype(jnp.bfloat16))
                if with_key:
                    parts.append(k_ref[rows_of(step), lanes[pair]])
                batch[pair] = jnp.concatenate(parts, axis=0) if len(parts) > 1 else parts[0]
            for pair, side in sides:
                value[pair, side] = dot_nn(batch[pair], w1_s[2 * pair + side])
            for at in sides:
                v = value[at]
                square, bent = gelu_parts(v)
                doubled[at] = (v + v * bent).astype(jnp.bfloat16)
                if with_key:
                    v, s, b = v[-MINI:], square[-MINI:], bent[-MINI:]
                    slope[at] = (1.0 + b) + v * (1.0 - b * b) * (3.0 * gelu_b * s + gelu_a)
            for pair in group:
                total[pair] = dot_nt(doubled[pair, 0], w2_s[2 * pair]) + dot_nt(
                    doubled[pair, 1], w2_s[2 * pair + 1]
                )
            count = batch[group[0]].shape[0]
            squares = jnp.concatenate([(total[pair] * total[pair]).astype(jnp.bfloat16) for pair in group], axis=0)
            spread = dot_nn(squares, block_ones)
            for at, pair in enumerate(group):
                part = spread[at * count : (at + 1) * count]
                inverse[pair] = lax.rsqrt(part * (1.0 / half) + 4.0 * norm_epsilon)
                unit[pair] = total[pair] * inverse[pair]
            if with_query:
                for pair in group:
                    query = q_ref[rows_of(step - 1), lanes[pair]]
                    out_ref[rows_of(step - 1), lanes[pair]] = (query + unit[pair][:MINI]).astype(jnp.bfloat16)
            if not with_key:
                continue
            rows = rows_of(step)
            grads = {}
            for pair in group:
                grads[pair] = e_ref[rows, lanes[pair]] * (unit[pair][-MINI:] - t_ref[rows, lanes[pair]])
            products = [(grads[pair] * unit[pair][-MINI:]).astype(jnp.bfloat16) for pair in group]
            along = dot_nn(jnp.concatenate(products, axis=0), block_ones) * (1.0 / half)
            for at, pair in enumerate(group):
                part = along[at * MINI : (at + 1) * MINI]
                change[pair] = (
                    inverse[pair][-MINI:] * (grads[pair] - unit[pair][-MINI:] * part)
                ).astype(jnp.bfloat16)
            back = {}
            for pair, side in sides:
                back[pair, side] = (dot_nn(change[pair], w2_s[2 * pair + side]) * slope[pair, side]).astype(jnp.bfloat16)
            for pair, side in sides:
                head = 2 * pair + side
                here = slice(side * half, side * half + half)
                w2 = w2_out[head] - dot_nn(change[pair].T[here], doubled[pair, side][-MINI:])
                w2_out[head] = w2
                w2_s[head, here, :] = w2.astype(jnp.bfloat16)
                w1 = w1_out[head] - dot_nn(k_ref[rows, lanes[pair]].T[here], back[pair, side])
                w1_out[head] = w1
                w1_s[head, here, :] = w1.astype(jnp.bfloat16)

    one(0, False, True)
    lax.fori_loop(1, steps, lambda step, carry: (one(step, True, True), carry)[1], 0)
    one(steps, True, False)


def run_chunk(shards, rates, weight, row_blocks, w1, w2, half, after=()):
    shards = [shard for shard in shards if shard is not None]
    tokens, depth = shards[0].shape
    heads, _, hidden = w1.shape
    inputs = len(shards)
    count = weight.shape[0] // depth
    state = jax.ShapeDtypeStruct(w1.shape, jnp.float32)
    inside = pl.BlockSpec(memory_space=pltpu.VMEM)
    wide = pltpu.VMEM((tokens, heads * half), jnp.float32)
    return pl.pallas_call(
        functools.partial(chunk_kernel, inputs=inputs, shards=count, half=half, extra=len(after)),
        in_specs=[pl.BlockSpec(memory_space=pltpu.SMEM)]
        + [inside] * (inputs + 4)
        + [pl.BlockSpec(memory_space=pl.ANY)] * len(after),
        out_specs=[inside] * 3,
        out_shape=[jax.ShapeDtypeStruct((tokens, heads * half), jnp.bfloat16), state, state],
        scratch_shapes=[
            pltpu.VMEM((tokens, count * depth), jnp.bfloat16),
            wide,
            pltpu.VMEM((tokens, heads * half), jnp.bfloat16),
            wide,
            wide,
            pltpu.VMEM((heads, 2 * half, hidden), jnp.bfloat16),
            pltpu.VMEM((heads, 2 * half, hidden), jnp.bfloat16),
        ],
        compiler_params=pltpu.CompilerParams(vmem_limit_bytes=CHUNK_VMEM),
        name="fast_weights",
    )(row_blocks, *shards, rates, weight, w1, w2, *after)


def normalize(values):
    center = values - jnp.mean(values, axis=-1, keepdims=True)
    spread = jnp.mean(center * center, axis=-1, keepdims=True)
    return center * lax.rsqrt(spread + norm_epsilon)


def fast_mlp(inputs, fast_weights):
    hidden = jax.nn.gelu(
        jnp.einsum("bmd,bdf->bmf", inputs, fast_weights[:, 0], precision=highest_precision),
        approximate=True,
    )
    return normalize(
        jnp.einsum("bmf,bdf->bmd", hidden, fast_weights[:, 1], precision=highest_precision)
    )


def minibatch(fast_weights, batch_items):
    queries, key_rows, value_rows, step_rates = batch_items
    target = value_rows - key_rows

    def loss_value(weights_now):
        error = fast_mlp(key_rows, weights_now) - target
        return 0.5 * jnp.sum(step_rates[:, :, None] * error * error) / step_rates.shape[-1]

    gradient = jax.grad(loss_value)(fast_weights)
    fast_weights = fast_weights - gradient
    return (fast_weights, queries + fast_mlp(queries, fast_weights))


def run_items(fast_weights, picked, step_rates):
    batch = picked.shape[0]
    seg_len = picked.shape[2]
    head_dim = picked.shape[3]
    block_count = seg_len // MINI

    def to_blocks(array):
        return array.reshape(batch, block_count, MINI, head_dim).transpose(1, 0, 2, 3)

    rate_blocks = step_rates.reshape(batch, block_count, MINI).transpose(1, 0, 2)
    fast_weights, outputs = lax.scan(
        minibatch,
        fast_weights,
        (to_blocks(picked[:, 0]), to_blocks(picked[:, 1]), to_blocks(picked[:, 2]), rate_blocks),
    )
    return (fast_weights, outputs.transpose(1, 0, 2, 3).reshape(batch, seg_len, head_dim))


def any_size(attn_query, attn_key, attn_value, prompt_len, ttt_weight, init_w1, init_w2t, step_rate):
    videos = attn_query.shape[0]
    seg_len = attn_query.shape[1]
    heads_dev = init_w1.shape[0]
    head_dim = init_w1.shape[1]
    position = lax.broadcasted_iota(jnp.int32, (videos, seg_len), 1)
    usable = (position >= TEXT_SLOTS) | (position < prompt_len)
    queries = attn_query.reshape(videos, seg_len, heads_dev, head_dim)
    key_rows = attn_key.reshape(videos, seg_len, heads_dev, head_dim)
    value_rows = attn_value.reshape(videos, seg_len, heads_dev, head_dim)
    scores = jnp.einsum(
        "vqhd,vkhd->vhqk", queries, key_rows, preferred_element_type=jnp.float32
    ) * head_dim ** (-0.5)
    scores = jnp.where(usable[:, None, None, :], scores, -1e30)
    largest = jnp.max(scores, axis=-1, keepdims=True)
    exponent = jnp.exp(scores - largest)
    weights = (exponent / jnp.sum(exponent, axis=-1, keepdims=True)).astype(jnp.bfloat16)
    attended = jnp.einsum(
        "vhqk,vkhd->vqhd", weights, value_rows, preferred_element_type=jnp.float32
    )
    attended = attended.astype(jnp.bfloat16).reshape(videos, seg_len, heads_dev * head_dim)
    features = lax.all_gather(attended, "head", axis=2, tiled=True)
    feature_full = features.astype(jnp.float32)
    normed = (
        feature_full
        * lax.rsqrt(jnp.mean(feature_full * feature_full, axis=-1, keepdims=True) + rms_epsilon)
    ).astype(jnp.bfloat16)
    projected = jnp.dot(
        normed.reshape(videos * seg_len, normed.shape[2]),
        ttt_weight,
        preferred_element_type=jnp.float32,
    )
    projected = projected.reshape(videos, seg_len, heads_dev, 3, head_dim).transpose(0, 2, 3, 1, 4)
    step_rates = step_rate * usable[:, None, :].astype(jnp.float32)
    init_stack = jnp.stack([init_w1, init_w2t], axis=1)
    seg_count = lax.axis_size("seg")
    item_count = videos * heads_dev
    per_device = (item_count + seg_count - 1) // seg_count
    padded = per_device * seg_count
    item_inputs = projected.reshape(item_count, 3, seg_len, head_dim)
    item_inputs = jnp.pad(item_inputs, ((0, padded - item_count), (0, 0), (0, 0), (0, 0)))
    item_rates = step_rates.reshape(item_count, 1, seg_len, 1)
    item_rates = jnp.pad(item_rates, ((0, padded - item_count), (0, 0), (0, 0), (0, 0)))
    sequences, rate_rows = (
        lax.all_to_all(
            item_inputs.astype(jnp.bfloat16), "seg", split_axis=0, concat_axis=2, tiled=True
        ).astype(item_inputs.dtype),
        lax.all_to_all(
            item_rates.astype(jnp.bfloat16), "seg", split_axis=0, concat_axis=2, tiled=True
        ).astype(item_rates.dtype),
    )
    item_global = lax.axis_index("seg") * per_device + jnp.arange(per_device, dtype=jnp.int32)
    head_of = item_global % heads_dev
    start = jnp.take(init_stack, head_of, axis=0)
    final_weights, outputs = run_items(
        start, sequences, rate_rows.reshape(per_device, sequences.shape[2])
    )
    returned = lax.all_to_all(
        outputs.astype(jnp.bfloat16), "seg", split_axis=1, concat_axis=0, tiled=True
    ).astype(outputs.dtype)
    results = returned[:item_count].reshape(videos, heads_dev, seg_len, head_dim)
    results = results.transpose(0, 2, 1, 3).reshape(videos, seg_len, heads_dev * head_dim)
    return results.astype(jnp.bfloat16)


def take_kernel(*refs, at):
    out = refs[-1]
    out[...] = refs[0][at : at + out.shape[0], : out.shape[1]]


def take(source, at, rows, columns, after):
    return pl.pallas_call(
        functools.partial(take_kernel, at=at),
        in_specs=[pl.BlockSpec(memory_space=pltpu.VMEM)]
        + [pl.BlockSpec(memory_space=pl.ANY)] * len(after),
        out_specs=pl.BlockSpec(memory_space=pltpu.VMEM),
        out_shape=jax.ShapeDtypeStruct((rows, columns), source.dtype),
        compiler_params=pltpu.CompilerParams(vmem_limit_bytes=8 * 1024 * 1024),
        name="take",
    )(source, *after)


CHUNK_PARTS = (4, 4, 4, 4)
FAR_GATE = 1
OUT_GATE = 3
KG = 1
DIRECT = ()


def chunk_sizes(tokens):
    if tokens % (16 * MINI):
        return [tokens]
    return [part * (tokens // 16) for part in CHUNK_PARTS]


NEAR = [(0, 1), (1, 0), (2, 3), (3, 2)]
FAR = [(0, 2), (2, 0), (1, 3), (3, 1)]
INNER = [(1, 2), (2, 1)]
OUTER = [(2, 3), (1, 0)]
ACROSS = [(0, 3), (3, 0), (1, 2), (2, 1)]


def by_video(attn_query, attn_key, attn_value, prompt_len, ttt_weight, init_w1, init_w2t, step_rate):
    videos, seg_len, channels = attn_query.shape
    half = init_w1.shape[1]
    segments = lax.axis_size("seg")
    mixed = attention(attn_query, attn_key, attn_value, prompt_len[:, 0], step_rate, half)
    mine = lax.all_to_all(mixed, "seg", split_axis=0, concat_axis=0, tiled=True)
    mine = mine.reshape(segments * seg_len, mixed.shape[2])
    rates = mine[:, channels:]
    w1 = init_w1
    w2 = init_w2t - jnp.mean(init_w2t, axis=1, keepdims=True)
    tokens = segments * seg_len
    chunk = tokens // 4
    count = lax.axis_size("head")
    me = lax.axis_index("head")
    row_blocks = me ^ jnp.arange(4, dtype=jnp.int32)
    sizes = chunk_sizes(tokens)
    ends = [sum(sizes[: c + 1]) for c in range(len(sizes))]
    blocks, pieces, outs = [], [], []

    def send(c):
        at, size = ends[c] - sizes[c], sizes[c]
        after = []
        if c >= FAR_GATE:
            after.append(pieces[c - FAR_GATE][0])
        if c >= OUT_GATE:
            after.append(outs[c - OUT_GATE])
        block = take(mine, at, size, channels, after)
        far = lax.ppermute(block, "head", FAR)
        near = lax.ppermute(block, "head", NEAR)
        if c in DIRECT:
            pieces.append((far, near, lax.ppermute(block, "head", ACROSS), None))
        else:
            inner = lax.ppermute(block, "head", INNER)
            outer = lax.ppermute(far, "head", OUTER)
            pieces.append((far, near, inner, outer))
        blocks.append(block)

    for c in range(min(OUT_GATE, len(sizes))):
        send(c)
    for c in range(len(sizes)):
        far, near, inner, outer = pieces[c]
        rate = rates[ends[c] - sizes[c] : ends[c]]
        after = [blocks[c + KG]] if c + KG < len(blocks) else []
        shards = [blocks[c], near, far, inner, outer]
        out, w1, w2 = run_chunk(shards, rate, ttt_weight, row_blocks, w1, w2, half, after)
        outs.append(out)
        if c + OUT_GATE < len(sizes):
            send(c + OUT_GATE)
    result = jnp.concatenate(outs, axis=0).reshape(videos, seg_len, channels)
    return lax.all_to_all(result, "seg", split_axis=0, concat_axis=0, tiled=True)


def body(attn_query, attn_key, attn_value, prompt_len, ttt_weight, init_w1, init_w2t, step_rate):
    videos, seg_len, channels = attn_query.shape
    heads, half, hidden = init_w1.shape
    whole_pairs = heads % 2 == 0 and 2 * half == 128 and hidden % 128 == 0
    fits = seg_len % 128 == 0 and heads <= 128
    run = by_video if videos == lax.axis_size("seg") and whole_pairs and fits and lax.axis_size("head") == 4 else any_size
    return run(attn_query, attn_key, attn_value, prompt_len, ttt_weight, init_w1, init_w2t, step_rate)


def solution(mesh):
    return jax.shard_map(
        body,
        mesh=mesh,
        in_specs=(
            P(None, "seg", "head"),
            P(None, "seg", "head"),
            P(None, "seg", "head"),
            P(None, "seg"),
            P(None, "head"),
            P("head", None, None),
            P("head", None, None),
            P(None, "head", "seg"),
        ),
        out_specs=P(None, "seg", "head"),
        check_vma=False,
    )
```

```python
import functools
import jax
import jax.numpy as jnp
from jax import lax
from jax.experimental import pallas as pl
from jax.experimental.pallas import tpu as pltpu
from jax.sharding import PartitionSpec as P

highest_precision = lax.Precision.HIGHEST
MINI = 64
TEXT_SLOTS = 64
norm_epsilon = 1e-05
rms_epsilon = 1e-06
GROUP = 6
PB = 3
VIDEO_STEP = 2
CHUNK_VMEM = 26 * 1024 * 1024
VMEM_LIMIT = 20 * 1024 * 1024
gelu_a = 0.7978845608028654
gelu_b = gelu_a * 0.044715


def dot_nn(a, b):
    return lax.dot_general(a, b, (((1,), (0,)), ((), ())), preferred_element_type=jnp.float32)


def dot_nt(a, b):
    return lax.dot_general(a, b, (((1,), (1,)), ((), ())), preferred_element_type=jnp.float32)


def low_half(shape, half):
    return lax.broadcasted_iota(jnp.int32, shape, len(shape) - 1) < half


def half_ones(half):
    width = 2 * half
    row = lax.broadcasted_iota(jnp.int32, (width, width), 0) < half
    column = lax.broadcasted_iota(jnp.int32, (width, width), 1) < half
    return (row == column).astype(jnp.bfloat16)


def attention_kernel(lens_ref, q_ref, k_ref, v_ref, rate_ref, out_ref, *, half):
    videos = q_ref.shape[0]
    seg_len = q_ref.shape[1]
    channels = q_ref.shape[2]
    width = 2 * half
    heads = channels // half
    key_at = lax.broadcasted_iota(jnp.int32, (seg_len, 2 * seg_len), 1)
    key_at = jnp.where(key_at >= seg_len, key_at - seg_len, key_at)
    low = low_half((seg_len, width), half)
    zero = jnp.zeros((seg_len, width), jnp.bfloat16)
    ones = jnp.ones((seg_len, width), jnp.bfloat16)
    scale = jnp.asarray(half ** (-0.5), jnp.bfloat16)
    totals = jnp.concatenate([jnp.where(low, ones, zero), jnp.where(low, zero, ones)], axis=0)
    for v in range(videos):
        length = lens_ref[pl.program_id(0) * videos + v]
        usable = (key_at >= TEXT_SLOTS) | (key_at < length)
        for pair in range(channels // width):
            lanes = slice(pair * width, (pair + 1) * width)
            query = q_ref[v, :, lanes] * scale
            key = k_ref[v, :, lanes]
            value = v_ref[v, :, lanes]
            keys = jnp.concatenate([jnp.where(low, key, zero), jnp.where(low, zero, key)], axis=0)
            scores = jnp.where(usable, dot_nt(query, keys), -1e30)
            parts = []
            for side in range(2):
                block = scores[:, side * seg_len : (side + 1) * seg_len]
                largest = jnp.max(block, axis=1, keepdims=True)
                parts.append(jnp.exp(block - largest).astype(jnp.bfloat16))
            weights = jnp.concatenate(parts, axis=1)
            values = jnp.concatenate([jnp.where(low, value, zero), jnp.where(low, zero, value)], axis=0)
            mixed = dot_nn(weights, jnp.concatenate([values, totals], axis=1))
            out_ref[v, :, lanes] = (mixed[:, :width] / mixed[:, width:]).astype(jnp.bfloat16)
        token = lax.broadcasted_iota(jnp.int32, (seg_len, 1), 0)
        open_token = ((token >= TEXT_SLOTS) | (token < length)).astype(jnp.float32)
        rates = rate_ref[v]
        spare = out_ref.shape[2] - channels
        rates = jnp.concatenate(
            [rates, jnp.zeros((spare - rates.shape[0], seg_len), jnp.float32)], axis=0
        )
        out_ref[v, :, channels:] = (rates.T * open_token).astype(jnp.bfloat16)


def attention(attn_query, attn_key, attn_value, lens, step_rate, half):
    videos, seg_len, channels = attn_query.shape
    heads = step_rate.shape[1]
    spare = 128
    step = VIDEO_STEP if videos % VIDEO_STEP == 0 else 1
    block = pl.BlockSpec((step, seg_len, channels), lambda v, lens: (v, 0, 0))
    return pl.pallas_call(
        functools.partial(attention_kernel, half=half),
        grid_spec=pltpu.PrefetchScalarGridSpec(
            num_scalar_prefetch=1,
            grid=(videos // step,),
            in_specs=[block, block, block, pl.BlockSpec((step, heads, seg_len), lambda v, lens: (v, 0, 0))],
            out_specs=pl.BlockSpec((step, seg_len, channels + spare), lambda v, lens: (v, 0, 0)),
        ),
        out_shape=jax.ShapeDtypeStruct((videos, seg_len, channels + spare), jnp.bfloat16),
        compiler_params=pltpu.CompilerParams(vmem_limit_bytes=58 * 1024 * 1024),
        name="attention",
    )(lens, attn_query, attn_key, attn_value, step_rate)


def chunk_kernel(row_ref, *refs, inputs, shards, half, extra):
    x_refs, refs = refs[:inputs], refs[inputs:]
    rate_ref, w_ref, w1_in, w2_in = refs[:4]
    out_ref, w1_out, w2_out = refs[4 + extra : 7 + extra]
    x_s, q_ref, k_ref, t_ref, e_ref, w1_s, w2_s = refs[7 + extra :]
    tokens, depth = x_refs[0].shape
    width = 2 * half
    steps = tokens // MINI
    pairs = q_ref.shape[1] // width
    hidden = w1_in.shape[2]
    block_ones = half_ones(half)

    w1_out[...] = w1_in[...]
    w2_out[...] = w2_in[...]
    for head in range(2 * pairs):
        here = slice((head % 2) * half, (head % 2) * half + half)
        other = slice(half - (head % 2) * half, 2 * half - (head % 2) * half)
        w1_s[head, here, :] = w1_in[head].astype(jnp.bfloat16)
        w1_s[head, other, :] = jnp.zeros((half, hidden), jnp.bfloat16)
        w2_s[head, here, :] = w2_in[head].astype(jnp.bfloat16)
        w2_s[head, other, :] = jnp.zeros((half, hidden), jnp.bfloat16)

    squares = jnp.zeros((tokens, 128), jnp.float32)
    for i in range(shards):
        source, rows = x_refs[min(i, 2)], slice(0, tokens) if i < 3 else slice(tokens, 2 * tokens)
        start = row_ref[i] * depth
        for at in range(0, depth, 128):
            piece = source[rows, at : at + 128]
            x_s[:, pl.ds(pl.multiple_of(start + at, 128), 128)] = piece
            wide = piece.astype(jnp.float32)
            squares = squares + wide * wide
    mean = jnp.sum(squares, axis=1, keepdims=True) / (shards * depth)
    inv = jnp.broadcast_to(lax.rsqrt(mean + rms_epsilon), (tokens, width))

    low = low_half((tokens, width), half)
    zero = jnp.zeros((tokens, width), jnp.float32)
    block = PB if pairs % PB == 0 else 1
    for group in range(0, pairs, block):
        wide = 3 * width * block
        acc = dot_nn(x_s[...], w_ref[:, group * 3 * width : group * 3 * width + wide])
        for at in range(block):
            first, middle, last = (
                acc[:, (3 * at + j) * width : (3 * at + j + 1) * width] * inv for j in range(3)
            )
            query = jnp.where(low, first, middle)
            key = pltpu.roll(jnp.where(low, last, first), half, 1)
            target = jnp.where(low, middle, last) - key
            total_low = jnp.sum(jnp.where(low, target, zero), axis=1, keepdims=True)
            total_high = jnp.sum(jnp.where(low, zero, target), axis=1, keepdims=True)
            target = target - jnp.where(low, total_low, total_high) * (1.0 / half)
            lanes = slice((group + at) * width, (group + at + 1) * width)
            q_ref[:, lanes] = query
            k_ref[:, lanes] = key.astype(jnp.bfloat16)
            t_ref[:, lanes] = target
    head = lax.broadcasted_iota(jnp.int32, (rate_ref.shape[1], pairs * width), 0)
    lane = lax.broadcasted_iota(jnp.int32, (rate_ref.shape[1], pairs * width), 1)
    spread_to = (lane // half == head).astype(jnp.bfloat16)
    e_ref[...] = dot_nn(rate_ref[...], spread_to) * (1.0 / MINI)

    def rows_of(step):
        return pl.ds(pl.multiple_of(step * MINI, MINI), MINI)

    def gelu_parts(value):
        square = value * value
        return square, jnp.tanh(value * (gelu_b * square + gelu_a))

    def one(step, with_query, with_key):
        for first in range(0, pairs, GROUP):
            group = range(first, min(first + GROUP, pairs))
            sides = [(pair, side) for pair in group for side in range(2)]
            lanes = {pair: slice(pair * width, (pair + 1) * width) for pair in group}
            batch, value, doubled, slope, total, inverse, unit, change = ({} for _ in range(8))
            for pair in group:
                parts = []
                if with_query:
                    parts.append(q_ref[rows_of(step - 1), lanes[pair]].astype(jnp.bfloat16))
                if with_key:
                    parts.append(k_ref[rows_of(step), lanes[pair]])
                batch[pair] = jnp.concatenate(parts, axis=0) if len(parts) > 1 else parts[0]
            for pair, side in sides:
                value[pair, side] = dot_nn(batch[pair], w1_s[2 * pair + side])
            for at in sides:
                v = value[at]
                square, bent = gelu_parts(v)
                doubled[at] = (v + v * bent).astype(jnp.bfloat16)
                if with_key:
                    v, s, b = v[-MINI:], square[-MINI:], bent[-MINI:]
                    slope[at] = (1.0 + b) + v * (1.0 - b * b) * (3.0 * gelu_b * s + gelu_a)
            for pair in group:
                total[pair] = dot_nt(doubled[pair, 0], w2_s[2 * pair]) + dot_nt(
                    doubled[pair, 1], w2_s[2 * pair + 1]
                )
            count = batch[group[0]].shape[0]
            squares = jnp.concatenate([(total[pair] * total[pair]).astype(jnp.bfloat16) for pair in group], axis=0)
            spread = dot_nn(squares, block_ones)
            for at, pair in enumerate(group):
                part = spread[at * count : (at + 1) * count]
                inverse[pair] = lax.rsqrt(part * (1.0 / half) + 4.0 * norm_epsilon)
                unit[pair] = total[pair] * inverse[pair]
            if with_query:
                for pair in group:
                    query = q_ref[rows_of(step - 1), lanes[pair]]
                    out_ref[rows_of(step - 1), lanes[pair]] = (query + unit[pair][:MINI]).astype(jnp.bfloat16)
            if not with_key:
                continue
            rows = rows_of(step)
            grads = {}
            for pair in group:
                grads[pair] = e_ref[rows, lanes[pair]] * (unit[pair][-MINI:] - t_ref[rows, lanes[pair]])
            products = [(grads[pair] * unit[pair][-MINI:]).astype(jnp.bfloat16) for pair in group]
            along = dot_nn(jnp.concatenate(products, axis=0), block_ones) * (1.0 / half)
            for at, pair in enumerate(group):
                part = along[at * MINI : (at + 1) * MINI]
                change[pair] = (
                    inverse[pair][-MINI:] * (grads[pair] - unit[pair][-MINI:] * part)
                ).astype(jnp.bfloat16)
            back = {}
            for pair, side in sides:
                back[pair, side] = (dot_nn(change[pair], w2_s[2 * pair + side]) * slope[pair, side]).astype(jnp.bfloat16)
            for pair, side in sides:
                head = 2 * pair + side
                here = slice(side * half, side * half + half)
                w2 = w2_out[head] - dot_nn(change[pair].T[here], doubled[pair, side][-MINI:])
                w2_out[head] = w2
                w2_s[head, here, :] = w2.astype(jnp.bfloat16)
                w1 = w1_out[head] - dot_nn(k_ref[rows, lanes[pair]].T[here], back[pair, side])
                w1_out[head] = w1
                w1_s[head, here, :] = w1.astype(jnp.bfloat16)

    one(0, False, True)
    lax.fori_loop(1, steps, lambda step, carry: (one(step, True, True), carry)[1], 0)
    one(steps, True, False)


def run_chunk(shards, rates, weight, row_blocks, w1, w2, half, after=()):
    tokens, depth = shards[0].shape
    heads, _, hidden = w1.shape
    inputs = len(shards)
    count = weight.shape[0] // depth
    state = jax.ShapeDtypeStruct(w1.shape, jnp.float32)
    inside = pl.BlockSpec(memory_space=pltpu.VMEM)
    wide = pltpu.VMEM((tokens, heads * half), jnp.float32)
    return pl.pallas_call(
        functools.partial(chunk_kernel, inputs=inputs, shards=count, half=half, extra=len(after)),
        in_specs=[pl.BlockSpec(memory_space=pltpu.SMEM)]
        + [inside] * (inputs + 4)
        + [pl.BlockSpec(memory_space=pl.ANY)] * len(after),
        out_specs=[inside] * 3,
        out_shape=[jax.ShapeDtypeStruct((tokens, heads * half), jnp.bfloat16), state, state],
        scratch_shapes=[
            pltpu.VMEM((tokens, count * depth), jnp.bfloat16),
            wide,
            pltpu.VMEM((tokens, heads * half), jnp.bfloat16),
            wide,
            wide,
            pltpu.VMEM((heads, 2 * half, hidden), jnp.bfloat16),
            pltpu.VMEM((heads, 2 * half, hidden), jnp.bfloat16),
        ],
        compiler_params=pltpu.CompilerParams(vmem_limit_bytes=CHUNK_VMEM),
        name="fast_weights",
    )(row_blocks, *shards, rates, weight, w1, w2, *after)


def normalize(values):
    center = values - jnp.mean(values, axis=-1, keepdims=True)
    spread = jnp.mean(center * center, axis=-1, keepdims=True)
    return center * lax.rsqrt(spread + norm_epsilon)


def fast_mlp(inputs, fast_weights):
    hidden = jax.nn.gelu(
        jnp.einsum("bmd,bdf->bmf", inputs, fast_weights[:, 0], precision=highest_precision),
        approximate=True,
    )
    return normalize(
        jnp.einsum("bmf,bdf->bmd", hidden, fast_weights[:, 1], precision=highest_precision)
    )


def minibatch(fast_weights, batch_items):
    queries, key_rows, value_rows, step_rates = batch_items
    target = value_rows - key_rows

    def loss_value(weights_now):
        error = fast_mlp(key_rows, weights_now) - target
        return 0.5 * jnp.sum(step_rates[:, :, None] * error * error) / step_rates.shape[-1]

    gradient = jax.grad(loss_value)(fast_weights)
    fast_weights = fast_weights - gradient
    return (fast_weights, queries + fast_mlp(queries, fast_weights))


def run_items(fast_weights, picked, step_rates):
    batch = picked.shape[0]
    seg_len = picked.shape[2]
    head_dim = picked.shape[3]
    block_count = seg_len // MINI

    def to_blocks(array):
        return array.reshape(batch, block_count, MINI, head_dim).transpose(1, 0, 2, 3)

    rate_blocks = step_rates.reshape(batch, block_count, MINI).transpose(1, 0, 2)
    fast_weights, outputs = lax.scan(
        minibatch,
        fast_weights,
        (to_blocks(picked[:, 0]), to_blocks(picked[:, 1]), to_blocks(picked[:, 2]), rate_blocks),
    )
    return (fast_weights, outputs.transpose(1, 0, 2, 3).reshape(batch, seg_len, head_dim))


def any_size(attn_query, attn_key, attn_value, prompt_len, ttt_weight, init_w1, init_w2t, step_rate):
    videos = attn_query.shape[0]
    seg_len = attn_query.shape[1]
    heads_dev = init_w1.shape[0]
    head_dim = init_w1.shape[1]
    position = lax.broadcasted_iota(jnp.int32, (videos, seg_len), 1)
    usable = (position >= TEXT_SLOTS) | (position < prompt_len)
    queries = attn_query.reshape(videos, seg_len, heads_dev, head_dim)
    key_rows = attn_key.reshape(videos, seg_len, heads_dev, head_dim)
    value_rows = attn_value.reshape(videos, seg_len, heads_dev, head_dim)
    scores = jnp.einsum(
        "vqhd,vkhd->vhqk", queries, key_rows, preferred_element_type=jnp.float32
    ) * head_dim ** (-0.5)
    scores = jnp.where(usable[:, None, None, :], scores, -1e30)
    largest = jnp.max(scores, axis=-1, keepdims=True)
    exponent = jnp.exp(scores - largest)
    weights = (exponent / jnp.sum(exponent, axis=-1, keepdims=True)).astype(jnp.bfloat16)
    attended = jnp.einsum(
        "vhqk,vkhd->vqhd", weights, value_rows, preferred_element_type=jnp.float32
    )
    attended = attended.astype(jnp.bfloat16).reshape(videos, seg_len, heads_dev * head_dim)
    features = lax.all_gather(attended, "head", axis=2, tiled=True)
    feature_full = features.astype(jnp.float32)
    normed = (
        feature_full
        * lax.rsqrt(jnp.mean(feature_full * feature_full, axis=-1, keepdims=True) + rms_epsilon)
    ).astype(jnp.bfloat16)
    projected = jnp.dot(
        normed.reshape(videos * seg_len, normed.shape[2]),
        ttt_weight,
        preferred_element_type=jnp.float32,
    )
    projected = projected.reshape(videos, seg_len, heads_dev, 3, head_dim).transpose(0, 2, 3, 1, 4)
    step_rates = step_rate * usable[:, None, :].astype(jnp.float32)
    init_stack = jnp.stack([init_w1, init_w2t], axis=1)
    seg_count = lax.axis_size("seg")
    item_count = videos * heads_dev
    per_device = (item_count + seg_count - 1) // seg_count
    padded = per_device * seg_count
    item_inputs = projected.reshape(item_count, 3, seg_len, head_dim)
    item_inputs = jnp.pad(item_inputs, ((0, padded - item_count), (0, 0), (0, 0), (0, 0)))
    item_rates = step_rates.reshape(item_count, 1, seg_len, 1)
    item_rates = jnp.pad(item_rates, ((0, padded - item_count), (0, 0), (0, 0), (0, 0)))
    sequences, rate_rows = (
        lax.all_to_all(
            item_inputs.astype(jnp.bfloat16), "seg", split_axis=0, concat_axis=2, tiled=True
        ).astype(item_inputs.dtype),
        lax.all_to_all(
            item_rates.astype(jnp.bfloat16), "seg", split_axis=0, concat_axis=2, tiled=True
        ).astype(item_rates.dtype),
    )
    item_global = lax.axis_index("seg") * per_device + jnp.arange(per_device, dtype=jnp.int32)
    head_of = item_global % heads_dev
    start = jnp.take(init_stack, head_of, axis=0)
    final_weights, outputs = run_items(
        start, sequences, rate_rows.reshape(per_device, sequences.shape[2])
    )
    returned = lax.all_to_all(
        outputs.astype(jnp.bfloat16), "seg", split_axis=1, concat_axis=0, tiled=True
    ).astype(outputs.dtype)
    results = returned[:item_count].reshape(videos, heads_dev, seg_len, head_dim)
    results = results.transpose(0, 2, 1, 3).reshape(videos, seg_len, heads_dev * head_dim)
    return results.astype(jnp.bfloat16)


def take_kernel(*refs, at, rows):
    out = refs[-1]
    out[:rows] = refs[0][at : at + rows, : out.shape[1]]
    if out.shape[0] > rows:
        out[rows:] = refs[1][...]


def take(source, at, rows, columns, second=None, after=(), beside=()):
    inputs = [source] if second is None else [source, second]
    return pl.pallas_call(
        functools.partial(take_kernel, at=at, rows=rows),
        in_specs=[pl.BlockSpec(memory_space=pltpu.VMEM)] * len(inputs)
        + [pl.BlockSpec(memory_space=pltpu.VMEM)] * len(beside)
        + [pl.BlockSpec(memory_space=pl.ANY)] * len(after),
        out_specs=pl.BlockSpec(memory_space=pltpu.VMEM),
        out_shape=jax.ShapeDtypeStruct((rows * len(inputs), columns), source.dtype),
        cost_estimate=pl.CostEstimate(flops=1, transcendentals=0, bytes_accessed=1),
        compiler_params=pltpu.CompilerParams(vmem_limit_bytes=8 * 1024 * 1024),
        name="take",
    )(*inputs, *beside, *after)


CHUNK_PARTS = (3, 4, 4, 3, 2)
LAG = 2
AHEAD = 2
WAT = 0


def chunk_sizes(tokens):
    if tokens % (16 * MINI):
        return [tokens]
    return [part * (tokens // 16) for part in CHUNK_PARTS]


NEAR = [(0, 1), (1, 0), (2, 3), (3, 2)]
FAR = [(0, 2), (2, 0), (1, 3), (3, 1)]


def by_video(attn_query, attn_key, attn_value, prompt_len, ttt_weight, init_w1, init_w2t, step_rate):
    videos, seg_len, channels = attn_query.shape
    half = init_w1.shape[1]
    segments = lax.axis_size("seg")
    mixed = attention(attn_query, attn_key, attn_value, prompt_len[:, 0], step_rate, half)
    mine = lax.all_to_all(mixed, "seg", split_axis=0, concat_axis=0, tiled=True)
    mine = mine.reshape(segments * seg_len, mixed.shape[2])
    rates = mine[:, channels:]
    w1 = init_w1
    w2 = init_w2t - jnp.mean(init_w2t, axis=1, keepdims=True)
    tokens = segments * seg_len
    chunk = tokens // 4
    count = lax.axis_size("head")
    me = lax.axis_index("head")
    row_blocks = me ^ jnp.array([0, 2, 1, 3], jnp.int32)
    sizes = chunk_sizes(tokens)
    ends = [sum(sizes[: c + 1]) for c in range(len(sizes))]
    chunks = len(sizes)
    outs, own, far, near = [], [], [], []

    def send_far(c, after):
        own.append(take(mine, ends[c] - sizes[c], sizes[c], channels, after=after))
        far.append(lax.ppermute(own[c], "head", FAR))

    def send_near(c, after):
        both = take(own[c], 0, sizes[c], channels, far[c], after, [ttt_weight] if c == WAT else [])
        near.append(lax.ppermute(both, "head", NEAR))
        return both

    for c in range(min(AHEAD, chunks)):
        send_far(c, [])
    for c in range(chunks + 1):
        if c < chunks:
            both = send_near(c, [outs[c - LAG]] if c >= LAG else [])
        if c + AHEAD < chunks:
            send_far(c + AHEAD, [both])
        if c > 0:
            d = c - 1
            after = [own[c + AHEAD]] if c + AHEAD < chunks else [both] if c < chunks else []
            rate = rates[ends[d] - sizes[d] : ends[d]]
            out, w1, w2 = run_chunk(
                [own[d], far[d], near[d]], rate, ttt_weight, row_blocks, w1, w2, half, after
            )
            outs.append(out)
    result = jnp.concatenate(outs, axis=0).reshape(videos, seg_len, channels)
    return lax.all_to_all(result, "seg", split_axis=0, concat_axis=0, tiled=True)


def body(attn_query, attn_key, attn_value, prompt_len, ttt_weight, init_w1, init_w2t, step_rate):
    videos, seg_len, channels = attn_query.shape
    heads, half, hidden = init_w1.shape
    whole_pairs = heads % 2 == 0 and 2 * half == 128 and hidden % 128 == 0
    fits = seg_len % 128 == 0 and heads <= 128
    run = by_video if videos == lax.axis_size("seg") and whole_pairs and fits and lax.axis_size("head") == 4 else any_size
    return run(attn_query, attn_key, attn_value, prompt_len, ttt_weight, init_w1, init_w2t, step_rate)


def solution(mesh):
    return jax.shard_map(
        body,
        mesh=mesh,
        in_specs=(
            P(None, "seg", "head"),
            P(None, "seg", "head"),
            P(None, "seg", "head"),
            P(None, "seg"),
            P(None, "head"),
            P("head", None, None),
            P("head", None, None),
            P(None, "head", "seg"),
        ),
        out_specs=P(None, "seg", "head"),
        check_vma=False,
    )
```

```python
import functools
import jax
import jax.numpy as jnp
from jax import lax
from jax.experimental import pallas as pl
from jax.experimental.pallas import tpu as pltpu
from jax.sharding import PartitionSpec as P

highest_precision = lax.Precision.HIGHEST
MINI = 64
TEXT_SLOTS = 64
norm_epsilon = 1e-05
rms_epsilon = 1e-06
GROUP = 6
PB = 3
VIDEO_STEP = 2
CHUNK_VMEM = 26 * 1024 * 1024
VMEM_LIMIT = 20 * 1024 * 1024
gelu_a = 0.7978845608028654
gelu_b = gelu_a * 0.044715


def dot_nn(a, b):
    return lax.dot_general(a, b, (((1,), (0,)), ((), ())), preferred_element_type=jnp.float32)


def dot_nt(a, b):
    return lax.dot_general(a, b, (((1,), (1,)), ((), ())), preferred_element_type=jnp.float32)


def low_half(shape, half):
    return lax.broadcasted_iota(jnp.int32, shape, len(shape) - 1) < half


def half_ones(half):
    width = 2 * half
    row = lax.broadcasted_iota(jnp.int32, (width, width), 0) < half
    column = lax.broadcasted_iota(jnp.int32, (width, width), 1) < half
    return (row == column).astype(jnp.bfloat16)


def attention_kernel(lens_ref, q_ref, k_ref, v_ref, rate_ref, out_ref, *, half):
    videos = q_ref.shape[0]
    seg_len = q_ref.shape[1]
    channels = q_ref.shape[2]
    width = 2 * half
    heads = channels // half
    key_at = lax.broadcasted_iota(jnp.int32, (seg_len, 2 * seg_len), 1)
    key_at = jnp.where(key_at >= seg_len, key_at - seg_len, key_at)
    low = low_half((seg_len, width), half)
    zero = jnp.zeros((seg_len, width), jnp.bfloat16)
    ones = jnp.ones((seg_len, width), jnp.bfloat16)
    scale = jnp.asarray(half ** (-0.5), jnp.bfloat16)
    totals = jnp.concatenate([jnp.where(low, ones, zero), jnp.where(low, zero, ones)], axis=0)
    for v in range(videos):
        length = lens_ref[pl.program_id(0) * videos + v]
        usable = (key_at >= TEXT_SLOTS) | (key_at < length)
        for pair in range(channels // width):
            lanes = slice(pair * width, (pair + 1) * width)
            query = q_ref[v, :, lanes] * scale
            key = k_ref[v, :, lanes]
            value = v_ref[v, :, lanes]
            keys = jnp.concatenate([jnp.where(low, key, zero), jnp.where(low, zero, key)], axis=0)
            scores = jnp.where(usable, dot_nt(query, keys), -1e30)
            parts = []
            for side in range(2):
                block = scores[:, side * seg_len : (side + 1) * seg_len]
                largest = jnp.max(block, axis=1, keepdims=True)
                parts.append(jnp.exp(block - largest).astype(jnp.bfloat16))
            weights = jnp.concatenate(parts, axis=1)
            values = jnp.concatenate([jnp.where(low, value, zero), jnp.where(low, zero, value)], axis=0)
            mixed = dot_nn(weights, jnp.concatenate([values, totals], axis=1))
            out_ref[v, :, lanes] = (mixed[:, :width] / mixed[:, width:]).astype(jnp.bfloat16)
        token = lax.broadcasted_iota(jnp.int32, (seg_len, 1), 0)
        open_token = ((token >= TEXT_SLOTS) | (token < length)).astype(jnp.float32)
        rates = rate_ref[:, pl.program_id(0) * videos + v, :]
        spare = out_ref.shape[2] - channels
        rates = jnp.concatenate(
            [rates, jnp.zeros((spare - rates.shape[0], seg_len), jnp.float32)], axis=0
        )
        out_ref[v, :, channels:] = (rates.T * open_token).astype(jnp.bfloat16)


def attention(attn_query, attn_key, attn_value, lens, step_rate, half):
    videos, seg_len, channels = attn_query.shape
    heads = step_rate.shape[1]
    spare = 128
    step = VIDEO_STEP if videos % VIDEO_STEP == 0 else 1
    block = pl.BlockSpec((step, seg_len, channels), lambda v, lens: (v, 0, 0))
    return pl.pallas_call(
        functools.partial(attention_kernel, half=half),
        grid_spec=pltpu.PrefetchScalarGridSpec(
            num_scalar_prefetch=1,
            grid=(videos // step,),
            in_specs=[block, block, block, pl.BlockSpec((heads, videos, seg_len), lambda v, lens: (0, 0, 0))],
            out_specs=pl.BlockSpec((step, seg_len, channels + spare), lambda v, lens: (v, 0, 0)),
        ),
        out_shape=jax.ShapeDtypeStruct((videos, seg_len, channels + spare), jnp.bfloat16),
        compiler_params=pltpu.CompilerParams(vmem_limit_bytes=58 * 1024 * 1024),
        name="attention",
    )(lens, attn_query, attn_key, attn_value, step_rate.transpose(1, 0, 2))


def chunk_kernel(row_ref, *refs, inputs, shards, half, extra, first, last):
    x_refs, refs = refs[:inputs], refs[inputs:]
    rate_ref, w_ref, w1_in, w2_in, held_in = refs[:5]
    out_ref, w1_out, w2_out, held_out = refs[5 + extra : 9 + extra]
    x_s, q_ref, k_ref, t_ref, e_ref, w1_s, w2_s = refs[9 + extra :]
    tokens, depth = x_refs[0].shape
    width = 2 * half
    steps = tokens // MINI
    skip = 1 if first else 0
    pairs = q_ref.shape[1] // width
    hidden = w1_in.shape[2]
    block_ones = half_ones(half)

    w1_out[...] = w1_in[...]
    w2_out[...] = w2_in[...]
    for head in range(2 * pairs):
        here = slice((head % 2) * half, (head % 2) * half + half)
        other = slice(half - (head % 2) * half, 2 * half - (head % 2) * half)
        w1_s[head, here, :] = w1_in[head].astype(jnp.bfloat16)
        w1_s[head, other, :] = jnp.zeros((half, hidden), jnp.bfloat16)
        w2_s[head, here, :] = w2_in[head].astype(jnp.bfloat16)
        w2_s[head, other, :] = jnp.zeros((half, hidden), jnp.bfloat16)

    squares = jnp.zeros((tokens, 128), jnp.float32)
    for i in range(shards):
        source, rows = x_refs[min(i, 2)], slice(0, tokens) if i < 3 else slice(tokens, 2 * tokens)
        start = row_ref[i] * depth
        for at in range(0, depth, 128):
            piece = source[rows, at : at + 128]
            x_s[:, pl.ds(pl.multiple_of(start + at, 128), 128)] = piece
            wide = piece.astype(jnp.float32)
            squares = squares + wide * wide
    mean = jnp.sum(squares, axis=1, keepdims=True) / (shards * depth)
    inv = jnp.broadcast_to(lax.rsqrt(mean + rms_epsilon), (tokens, width))

    q_ref[:MINI] = held_in[...]
    low = low_half((tokens, width), half)
    zero = jnp.zeros((tokens, width), jnp.float32)
    block = PB if pairs % PB == 0 else 1
    for group in range(0, pairs, block):
        wide = 3 * width * block
        acc = dot_nn(x_s[...], w_ref[:, group * 3 * width : group * 3 * width + wide])
        for at in range(block):
            left, middle, right = (
                acc[:, (3 * at + j) * width : (3 * at + j + 1) * width] * inv for j in range(3)
            )
            query = jnp.where(low, left, middle)
            key = pltpu.roll(jnp.where(low, right, left), half, 1)
            target = jnp.where(low, middle, right) - key
            total_low = jnp.sum(jnp.where(low, target, zero), axis=1, keepdims=True)
            total_high = jnp.sum(jnp.where(low, zero, target), axis=1, keepdims=True)
            target = target - jnp.where(low, total_low, total_high) * (1.0 / half)
            lanes = slice((group + at) * width, (group + at + 1) * width)
            q_ref[MINI:, lanes] = query
            k_ref[:, lanes] = key.astype(jnp.bfloat16)
            t_ref[:, lanes] = target
    head = lax.broadcasted_iota(jnp.int32, (rate_ref.shape[1], pairs * width), 0)
    lane = lax.broadcasted_iota(jnp.int32, (rate_ref.shape[1], pairs * width), 1)
    spread_to = (lane // half == head).astype(jnp.bfloat16)
    e_ref[...] = dot_nn(rate_ref[...], spread_to) * (1.0 / MINI)

    def rows_of(step):
        return pl.ds(pl.multiple_of(step * MINI, MINI), MINI)

    def gelu_parts(value):
        square = value * value
        return square, jnp.tanh(value * (gelu_b * square + gelu_a))

    def one(step, with_query, with_key):
        for first in range(0, pairs, GROUP):
            group = range(first, min(first + GROUP, pairs))
            sides = [(pair, side) for pair in group for side in range(2)]
            lanes = {pair: slice(pair * width, (pair + 1) * width) for pair in group}
            batch, value, doubled, slope, total, inverse, unit, change = ({} for _ in range(8))
            for pair in group:
                parts = []
                if with_query:
                    parts.append(q_ref[rows_of(step), lanes[pair]].astype(jnp.bfloat16))
                if with_key:
                    parts.append(k_ref[rows_of(step), lanes[pair]])
                batch[pair] = jnp.concatenate(parts, axis=0) if len(parts) > 1 else parts[0]
            for pair, side in sides:
                value[pair, side] = dot_nn(batch[pair], w1_s[2 * pair + side])
            for at in sides:
                v = value[at]
                square, bent = gelu_parts(v)
                doubled[at] = (v + v * bent).astype(jnp.bfloat16)
                if with_key:
                    v, s, b = v[-MINI:], square[-MINI:], bent[-MINI:]
                    slope[at] = (1.0 + b) + v * (1.0 - b * b) * (3.0 * gelu_b * s + gelu_a)
            for pair in group:
                total[pair] = dot_nt(doubled[pair, 0], w2_s[2 * pair]) + dot_nt(
                    doubled[pair, 1], w2_s[2 * pair + 1]
                )
            count = batch[group[0]].shape[0]
            squares = jnp.concatenate([(total[pair] * total[pair]).astype(jnp.bfloat16) for pair in group], axis=0)
            spread = dot_nn(squares, block_ones)
            for at, pair in enumerate(group):
                part = spread[at * count : (at + 1) * count]
                inverse[pair] = lax.rsqrt(part * (1.0 / half) + 4.0 * norm_epsilon)
                unit[pair] = total[pair] * inverse[pair]
            if with_query:
                for pair in group:
                    query = q_ref[rows_of(step), lanes[pair]]
                    out_ref[rows_of(step - skip), lanes[pair]] = (query + unit[pair][:MINI]).astype(jnp.bfloat16)
            if not with_key:
                continue
            rows = rows_of(step)
            grads = {}
            for pair in group:
                grads[pair] = e_ref[rows, lanes[pair]] * (unit[pair][-MINI:] - t_ref[rows, lanes[pair]])
            products = [(grads[pair] * unit[pair][-MINI:]).astype(jnp.bfloat16) for pair in group]
            along = dot_nn(jnp.concatenate(products, axis=0), block_ones) * (1.0 / half)
            for at, pair in enumerate(group):
                part = along[at * MINI : (at + 1) * MINI]
                change[pair] = (
                    inverse[pair][-MINI:] * (grads[pair] - unit[pair][-MINI:] * part)
                ).astype(jnp.bfloat16)
            back = {}
            for pair, side in sides:
                back[pair, side] = (dot_nn(change[pair], w2_s[2 * pair + side]) * slope[pair, side]).astype(jnp.bfloat16)
            for pair, side in sides:
                head = 2 * pair + side
                here = slice(side * half, side * half + half)
                w2 = w2_out[head] - dot_nn(change[pair].T[here], doubled[pair, side][-MINI:])
                w2_out[head] = w2
                w2_s[head, here, :] = w2.astype(jnp.bfloat16)
                w1 = w1_out[head] - dot_nn(k_ref[rows, lanes[pair]].T[here], back[pair, side])
                w1_out[head] = w1
                w1_s[head, here, :] = w1.astype(jnp.bfloat16)

    if first:
        one(0, False, True)
    lax.fori_loop(skip, steps, lambda step, carry: (one(step, True, True), carry)[1], 0)
    if last:
        one(steps, True, False)
    held_out[...] = q_ref[tokens:]


def run_chunk(shards, rates, weight, row_blocks, w1, w2, held, half, first, last, after=()):
    tokens, depth = shards[0].shape
    heads, _, hidden = w1.shape
    inputs = len(shards)
    count = weight.shape[0] // depth
    state = jax.ShapeDtypeStruct(w1.shape, jnp.float32)
    inside = pl.BlockSpec(memory_space=pltpu.VMEM)
    wide = pltpu.VMEM((tokens, heads * half), jnp.float32)
    return pl.pallas_call(
        functools.partial(chunk_kernel, inputs=inputs, shards=count, half=half, extra=len(after), first=first, last=last),
        in_specs=[pl.BlockSpec(memory_space=pltpu.SMEM)]
        + [inside] * (inputs + 5)
        + [pl.BlockSpec(memory_space=pl.ANY)] * len(after),
        out_specs=[inside] * 4,
        out_shape=[
            jax.ShapeDtypeStruct((tokens + MINI * (last - first), heads * half), jnp.bfloat16),
            state,
            state,
            jax.ShapeDtypeStruct((MINI, heads * half), jnp.float32),
        ],
        scratch_shapes=[
            pltpu.VMEM((tokens, count * depth), jnp.bfloat16),
            pltpu.VMEM((tokens + MINI, heads * half), jnp.float32),
            pltpu.VMEM((tokens, heads * half), jnp.bfloat16),
            wide,
            wide,
            pltpu.VMEM((heads, 2 * half, hidden), jnp.bfloat16),
            pltpu.VMEM((heads, 2 * half, hidden), jnp.bfloat16),
        ],
        compiler_params=pltpu.CompilerParams(vmem_limit_bytes=CHUNK_VMEM),
        name="fast_weights",
    )(row_blocks, *shards, rates, weight, w1, w2, held, *after)


def normalize(values):
    center = values - jnp.mean(values, axis=-1, keepdims=True)
    spread = jnp.mean(center * center, axis=-1, keepdims=True)
    return center * lax.rsqrt(spread + norm_epsilon)


def fast_mlp(inputs, fast_weights):
    hidden = jax.nn.gelu(
        jnp.einsum("bmd,bdf->bmf", inputs, fast_weights[:, 0], precision=highest_precision),
        approximate=True,
    )
    return normalize(
        jnp.einsum("bmf,bdf->bmd", hidden, fast_weights[:, 1], precision=highest_precision)
    )


def minibatch(fast_weights, batch_items):
    queries, key_rows, value_rows, step_rates = batch_items
    target = value_rows - key_rows

    def loss_value(weights_now):
        error = fast_mlp(key_rows, weights_now) - target
        return 0.5 * jnp.sum(step_rates[:, :, None] * error * error) / step_rates.shape[-1]

    gradient = jax.grad(loss_value)(fast_weights)
    fast_weights = fast_weights - gradient
    return (fast_weights, queries + fast_mlp(queries, fast_weights))


def run_items(fast_weights, picked, step_rates):
    batch = picked.shape[0]
    seg_len = picked.shape[2]
    head_dim = picked.shape[3]
    block_count = seg_len // MINI

    def to_blocks(array):
        return array.reshape(batch, block_count, MINI, head_dim).transpose(1, 0, 2, 3)

    rate_blocks = step_rates.reshape(batch, block_count, MINI).transpose(1, 0, 2)
    fast_weights, outputs = lax.scan(
        minibatch,
        fast_weights,
        (to_blocks(picked[:, 0]), to_blocks(picked[:, 1]), to_blocks(picked[:, 2]), rate_blocks),
    )
    return (fast_weights, outputs.transpose(1, 0, 2, 3).reshape(batch, seg_len, head_dim))


def any_size(attn_query, attn_key, attn_value, prompt_len, ttt_weight, init_w1, init_w2t, step_rate):
    videos = attn_query.shape[0]
    seg_len = attn_query.shape[1]
    heads_dev = init_w1.shape[0]
    head_dim = init_w1.shape[1]
    position = lax.broadcasted_iota(jnp.int32, (videos, seg_len), 1)
    usable = (position >= TEXT_SLOTS) | (position < prompt_len)
    queries = attn_query.reshape(videos, seg_len, heads_dev, head_dim)
    key_rows = attn_key.reshape(videos, seg_len, heads_dev, head_dim)
    value_rows = attn_value.reshape(videos, seg_len, heads_dev, head_dim)
    scores = jnp.einsum(
        "vqhd,vkhd->vhqk", queries, key_rows, preferred_element_type=jnp.float32
    ) * head_dim ** (-0.5)
    scores = jnp.where(usable[:, None, None, :], scores, -1e30)
    largest = jnp.max(scores, axis=-1, keepdims=True)
    exponent = jnp.exp(scores - largest)
    weights = (exponent / jnp.sum(exponent, axis=-1, keepdims=True)).astype(jnp.bfloat16)
    attended = jnp.einsum(
        "vhqk,vkhd->vqhd", weights, value_rows, preferred_element_type=jnp.float32
    )
    attended = attended.astype(jnp.bfloat16).reshape(videos, seg_len, heads_dev * head_dim)
    features = lax.all_gather(attended, "head", axis=2, tiled=True)
    feature_full = features.astype(jnp.float32)
    normed = (
        feature_full
        * lax.rsqrt(jnp.mean(feature_full * feature_full, axis=-1, keepdims=True) + rms_epsilon)
    ).astype(jnp.bfloat16)
    projected = jnp.dot(
        normed.reshape(videos * seg_len, normed.shape[2]),
        ttt_weight,
        preferred_element_type=jnp.float32,
    )
    projected = projected.reshape(videos, seg_len, heads_dev, 3, head_dim).transpose(0, 2, 3, 1, 4)
    step_rates = step_rate * usable[:, None, :].astype(jnp.float32)
    init_stack = jnp.stack([init_w1, init_w2t], axis=1)
    seg_count = lax.axis_size("seg")
    item_count = videos * heads_dev
    per_device = (item_count + seg_count - 1) // seg_count
    padded = per_device * seg_count
    item_inputs = projected.reshape(item_count, 3, seg_len, head_dim)
    item_inputs = jnp.pad(item_inputs, ((0, padded - item_count), (0, 0), (0, 0), (0, 0)))
    item_rates = step_rates.reshape(item_count, 1, seg_len, 1)
    item_rates = jnp.pad(item_rates, ((0, padded - item_count), (0, 0), (0, 0), (0, 0)))
    sequences, rate_rows = (
        lax.all_to_all(
            item_inputs.astype(jnp.bfloat16), "seg", split_axis=0, concat_axis=2, tiled=True
        ).astype(item_inputs.dtype),
        lax.all_to_all(
            item_rates.astype(jnp.bfloat16), "seg", split_axis=0, concat_axis=2, tiled=True
        ).astype(item_rates.dtype),
    )
    item_global = lax.axis_index("seg") * per_device + jnp.arange(per_device, dtype=jnp.int32)
    head_of = item_global % heads_dev
    start = jnp.take(init_stack, head_of, axis=0)
    final_weights, outputs = run_items(
        start, sequences, rate_rows.reshape(per_device, sequences.shape[2])
    )
    returned = lax.all_to_all(
        outputs.astype(jnp.bfloat16), "seg", split_axis=1, concat_axis=0, tiled=True
    ).astype(outputs.dtype)
    results = returned[:item_count].reshape(videos, heads_dev, seg_len, head_dim)
    results = results.transpose(0, 2, 1, 3).reshape(videos, seg_len, heads_dev * head_dim)
    return results.astype(jnp.bfloat16)


def take_kernel(*refs, at, rows):
    out = refs[-1]
    out[:rows] = refs[0][at : at + rows, : out.shape[1]]
    if out.shape[0] > rows:
        out[rows:] = refs[1][...]


def take(source, at, rows, columns, second=None, after=(), beside=()):
    inputs = [source] if second is None else [source, second]
    return pl.pallas_call(
        functools.partial(take_kernel, at=at, rows=rows),
        in_specs=[pl.BlockSpec(memory_space=pltpu.VMEM)] * len(inputs)
        + [pl.BlockSpec(memory_space=pltpu.VMEM)] * len(beside)
        + [pl.BlockSpec(memory_space=pl.ANY)] * len(after),
        out_specs=pl.BlockSpec(memory_space=pltpu.VMEM),
        out_shape=jax.ShapeDtypeStruct((rows * len(inputs), columns), source.dtype),
        cost_estimate=pl.CostEstimate(flops=1, transcendentals=0, bytes_accessed=1),
        compiler_params=pltpu.CompilerParams(vmem_limit_bytes=8 * 1024 * 1024),
        name="take",
    )(*inputs, *beside, *after)


CHUNK_PARTS = (3, 4, 4, 3, 2)
LAG = 2
AHEAD = 2
WAT = 2


def chunk_sizes(tokens):
    if tokens % (16 * MINI):
        return [tokens]
    return [part * (tokens // 16) for part in CHUNK_PARTS]


NEAR = [(0, 1), (1, 0), (2, 3), (3, 2)]
FAR = [(0, 2), (2, 0), (1, 3), (3, 1)]


def by_video(attn_query, attn_key, attn_value, prompt_len, ttt_weight, init_w1, init_w2t, step_rate):
    videos, seg_len, channels = attn_query.shape
    half = init_w1.shape[1]
    segments = lax.axis_size("seg")
    mixed = attention(attn_query, attn_key, attn_value, prompt_len[:, 0], step_rate, half)
    mine = lax.all_to_all(mixed, "seg", split_axis=0, concat_axis=0, tiled=True)
    mine = mine.reshape(segments * seg_len, mixed.shape[2])
    rates = mine[:, channels:]
    w1 = init_w1
    held = jnp.zeros((MINI, channels), jnp.float32)
    w2 = init_w2t - jnp.mean(init_w2t, axis=1, keepdims=True)
    tokens = segments * seg_len
    chunk = tokens // 4
    count = lax.axis_size("head")
    me = lax.axis_index("head")
    row_blocks = me ^ jnp.array([0, 2, 1, 3], jnp.int32)
    sizes = chunk_sizes(tokens)
    ends = [sum(sizes[: c + 1]) for c in range(len(sizes))]
    chunks = len(sizes)
    outs, own, far, near = [], [], [], []

    def send_far(c, after):
        own.append(take(mine, ends[c] - sizes[c], sizes[c], channels, after=after, beside=[ttt_weight] if c == WAT else []))
        far.append(lax.ppermute(own[c], "head", FAR))

    def send_near(c, after):
        both = take(own[c], 0, sizes[c], channels, far[c], after)
        near.append(lax.ppermute(both, "head", NEAR))
        return both

    for c in range(min(AHEAD, chunks)):
        send_far(c, [])
    for c in range(chunks + 1):
        if c < chunks:
            both = send_near(c, [outs[c - LAG]] if c >= LAG else [])
        if c + AHEAD < chunks:
            send_far(c + AHEAD, [both])
        if c > 0:
            d = c - 1
            after = [own[c + AHEAD]] if c + AHEAD < chunks else [both] if c < chunks else []
            rate = rates[ends[d] - sizes[d] : ends[d]]
            out, w1, w2, held = run_chunk(
                [own[d], far[d], near[d]], rate, ttt_weight, row_blocks, w1, w2, held, half, d == 0, d + 1 == chunks, after
            )
            outs.append(out)
    result = jnp.concatenate(outs, axis=0).reshape(videos, seg_len, channels)
    return lax.all_to_all(result, "seg", split_axis=0, concat_axis=0, tiled=True)


def body(attn_query, attn_key, attn_value, prompt_len, ttt_weight, init_w1, init_w2t, step_rate):
    videos, seg_len, channels = attn_query.shape
    heads, half, hidden = init_w1.shape
    whole_pairs = heads % 2 == 0 and 2 * half == 128 and hidden % 128 == 0
    fits = seg_len % 128 == 0 and heads <= 128
    run = by_video if videos == lax.axis_size("seg") and whole_pairs and fits and lax.axis_size("head") == 4 else any_size
    return run(attn_query, attn_key, attn_value, prompt_len, ttt_weight, init_w1, init_w2t, step_rate)


def solution(mesh):
    return jax.shard_map(
        body,
        mesh=mesh,
        in_specs=(
            P(None, "seg", "head"),
            P(None, "seg", "head"),
            P(None, "seg", "head"),
            P(None, "seg"),
            P(None, "head"),
            P("head", None, None),
            P("head", None, None),
            P(None, "head", "seg"),
        ),
        out_specs=P(None, "seg", "head"),
        check_vma=False,
    )
```

```python
import functools
import jax
import jax.numpy as jnp
from jax import lax
from jax.experimental import pallas as pl
from jax.experimental.pallas import tpu as pltpu
from jax.sharding import PartitionSpec as P

highest_precision = lax.Precision.HIGHEST
MINI = 64
TEXT_SLOTS = 64
norm_epsilon = 1e-05
rms_epsilon = 1e-06
GROUP = 6
PB = 3
VIDEO_STEP = 4
CHUNK_VMEM = 26 * 1024 * 1024
VMEM_LIMIT = 20 * 1024 * 1024
gelu_a = 0.7978845608028654
gelu_b = gelu_a * 0.044715


def dot_nn(a, b):
    return lax.dot_general(a, b, (((1,), (0,)), ((), ())), preferred_element_type=jnp.float32)


def dot_nt(a, b):
    return lax.dot_general(a, b, (((1,), (1,)), ((), ())), preferred_element_type=jnp.float32)


def low_half(shape, half):
    return lax.broadcasted_iota(jnp.int32, shape, len(shape) - 1) < half


def half_ones(half):
    width = 2 * half
    row = lax.broadcasted_iota(jnp.int32, (width, width), 0) < half
    column = lax.broadcasted_iota(jnp.int32, (width, width), 1) < half
    return (row == column).astype(jnp.bfloat16)


def attention_kernel(lens_ref, q_ref, k_ref, v_ref, rate_ref, out_ref, *, half):
    videos = q_ref.shape[0]
    seg_len = q_ref.shape[1]
    channels = q_ref.shape[2]
    width = 2 * half
    heads = channels // half
    key_at = lax.broadcasted_iota(jnp.int32, (seg_len, 2 * seg_len), 1)
    key_at = jnp.where(key_at >= seg_len, key_at - seg_len, key_at)
    low = low_half((seg_len, width), half)
    zero = jnp.zeros((seg_len, width), jnp.bfloat16)
    ones = jnp.ones((seg_len, width), jnp.bfloat16)
    scale = jnp.asarray(half ** (-0.5), jnp.bfloat16)
    totals = jnp.concatenate([jnp.where(low, ones, zero), jnp.where(low, zero, ones)], axis=0)
    for v in range(videos):
        length = lens_ref[pl.program_id(0) * videos + v]
        usable = (key_at >= TEXT_SLOTS) | (key_at < length)
        for pair in range(channels // width):
            lanes = slice(pair * width, (pair + 1) * width)
            query = q_ref[v, :, lanes] * scale
            key = k_ref[v, :, lanes]
            value = v_ref[v, :, lanes]
            keys = jnp.concatenate([jnp.where(low, key, zero), jnp.where(low, zero, key)], axis=0)
            scores = jnp.where(usable, dot_nt(query, keys), -1e30)
            parts = []
            for side in range(2):
                block = scores[:, side * seg_len : (side + 1) * seg_len]
                largest = jnp.max(block, axis=1, keepdims=True)
                parts.append(jnp.exp(block - largest).astype(jnp.bfloat16))
            weights = jnp.concatenate(parts, axis=1)
            values = jnp.concatenate([jnp.where(low, value, zero), jnp.where(low, zero, value)], axis=0)
            mixed = dot_nn(weights, jnp.concatenate([values, totals], axis=1))
            out_ref[v, :, lanes] = (mixed[:, :width] / mixed[:, width:]).astype(jnp.bfloat16)
        token = lax.broadcasted_iota(jnp.int32, (seg_len, 1), 0)
        open_token = ((token >= TEXT_SLOTS) | (token < length)).astype(jnp.float32)
        rates = rate_ref[:, pl.program_id(0) * videos + v, :]
        spare = out_ref.shape[2] - channels
        rates = jnp.concatenate(
            [rates, jnp.zeros((spare - rates.shape[0], seg_len), jnp.float32)], axis=0
        )
        out_ref[v, :, channels:] = (rates.T * open_token).astype(jnp.bfloat16)


def attention(attn_query, attn_key, attn_value, lens, step_rate, half):
    videos, seg_len, channels = attn_query.shape
    heads = step_rate.shape[1]
    spare = 128
    step = VIDEO_STEP if videos % VIDEO_STEP == 0 else 1
    block = pl.BlockSpec((step, seg_len, channels), lambda v, lens: (v, 0, 0))
    return pl.pallas_call(
        functools.partial(attention_kernel, half=half),
        grid_spec=pltpu.PrefetchScalarGridSpec(
            num_scalar_prefetch=1,
            grid=(videos // step,),
            in_specs=[block, block, block, pl.BlockSpec((heads, videos, seg_len), lambda v, lens: (0, 0, 0))],
            out_specs=pl.BlockSpec((step, seg_len, channels + spare), lambda v, lens: (v, 0, 0)),
        ),
        out_shape=jax.ShapeDtypeStruct((videos, seg_len, channels + spare), jnp.bfloat16),
        compiler_params=pltpu.CompilerParams(vmem_limit_bytes=58 * 1024 * 1024),
        name="attention",
    )(lens, attn_query, attn_key, attn_value, step_rate.transpose(1, 0, 2))


def chunk_kernel(row_ref, *refs, inputs, shards, half, extra, first, last):
    x_refs, refs = refs[:inputs], refs[inputs:]
    rate_ref, w_ref, w1_in, w2_in, held_in = refs[:5]
    out_ref, w1_out, w2_out, held_out = refs[5 + extra : 9 + extra]
    x_s, q_ref, k_ref, t_ref, e_ref, w1_s, w2_s = refs[9 + extra :]
    tokens, depth = x_refs[0].shape
    width = 2 * half
    steps = tokens // MINI
    skip = 1 if first else 0
    pairs = q_ref.shape[1] // width
    hidden = w1_in.shape[2]
    block_ones = half_ones(half)

    w1_out[...] = w1_in[...]
    w2_out[...] = w2_in[...]
    for head in range(2 * pairs):
        here = slice((head % 2) * half, (head % 2) * half + half)
        other = slice(half - (head % 2) * half, 2 * half - (head % 2) * half)
        w1_s[head, here, :] = w1_in[head].astype(jnp.bfloat16)
        w1_s[head, other, :] = jnp.zeros((half, hidden), jnp.bfloat16)
        w2_s[head, here, :] = w2_in[head].astype(jnp.bfloat16)
        w2_s[head, other, :] = jnp.zeros((half, hidden), jnp.bfloat16)

    squares = jnp.zeros((tokens, 128), jnp.float32)
    for i in range(shards):
        source, rows = x_refs[min(i, 2)], slice(0, tokens) if i < 3 else slice(tokens, 2 * tokens)
        start = row_ref[i] * depth
        for at in range(0, depth, 128):
            piece = source[rows, at : at + 128]
            x_s[:, pl.ds(pl.multiple_of(start + at, 128), 128)] = piece
            wide = piece.astype(jnp.float32)
            squares = squares + wide * wide
    mean = jnp.sum(squares, axis=1, keepdims=True) / (shards * depth)
    inv = jnp.broadcast_to(lax.rsqrt(mean + rms_epsilon), (tokens, width))

    q_ref[:MINI] = held_in[...]
    low = low_half((tokens, width), half)
    zero = jnp.zeros((tokens, width), jnp.float32)
    block = PB if pairs % PB == 0 else 1
    for group in range(0, pairs, block):
        wide = 3 * width * block
        acc = dot_nn(x_s[...], w_ref[:, group * 3 * width : group * 3 * width + wide])
        for at in range(block):
            left, middle, right = (
                acc[:, (3 * at + j) * width : (3 * at + j + 1) * width] * inv for j in range(3)
            )
            query = jnp.where(low, left, middle)
            key = pltpu.roll(jnp.where(low, right, left), half, 1)
            target = jnp.where(low, middle, right) - key
            total_low = jnp.sum(jnp.where(low, target, zero), axis=1, keepdims=True)
            total_high = jnp.sum(jnp.where(low, zero, target), axis=1, keepdims=True)
            target = target - jnp.where(low, total_low, total_high) * (1.0 / half)
            lanes = slice((group + at) * width, (group + at + 1) * width)
            q_ref[MINI:, lanes] = query
            k_ref[:, lanes] = key.astype(jnp.bfloat16)
            t_ref[:, lanes] = target
    head = lax.broadcasted_iota(jnp.int32, (rate_ref.shape[1], pairs * width), 0)
    lane = lax.broadcasted_iota(jnp.int32, (rate_ref.shape[1], pairs * width), 1)
    spread_to = (lane // half == head).astype(jnp.bfloat16)
    e_ref[...] = dot_nn(rate_ref[...], spread_to) * (1.0 / MINI)

    def rows_of(step):
        return pl.ds(pl.multiple_of(step * MINI, MINI), MINI)

    def gelu_parts(value):
        square = value * value
        return square, jnp.tanh(value * (gelu_b * square + gelu_a))

    def one(step, with_query, with_key):
        for first in range(0, pairs, GROUP):
            group = range(first, min(first + GROUP, pairs))
            sides = [(pair, side) for pair in group for side in range(2)]
            lanes = {pair: slice(pair * width, (pair + 1) * width) for pair in group}
            batch, value, doubled, slope, total, inverse, unit, change = ({} for _ in range(8))
            for pair in group:
                parts = []
                if with_query:
                    parts.append(q_ref[rows_of(step), lanes[pair]].astype(jnp.bfloat16))
                if with_key:
                    parts.append(k_ref[rows_of(step), lanes[pair]])
                batch[pair] = jnp.concatenate(parts, axis=0) if len(parts) > 1 else parts[0]
            for pair, side in sides:
                value[pair, side] = dot_nn(batch[pair], w1_s[2 * pair + side])
            for at in sides:
                v = value[at]
                square, bent = gelu_parts(v)
                doubled[at] = (v + v * bent).astype(jnp.bfloat16)
                if with_key:
                    v, s, b = v[-MINI:], square[-MINI:], bent[-MINI:]
                    slope[at] = (1.0 + b) + v * (1.0 - b * b) * (3.0 * gelu_b * s + gelu_a)
            for pair in group:
                total[pair] = dot_nt(doubled[pair, 0], w2_s[2 * pair]) + dot_nt(
                    doubled[pair, 1], w2_s[2 * pair + 1]
                )
            count = batch[group[0]].shape[0]
            squares = jnp.concatenate([(total[pair] * total[pair]).astype(jnp.bfloat16) for pair in group], axis=0)
            spread = dot_nn(squares, block_ones)
            for at, pair in enumerate(group):
                part = spread[at * count : (at + 1) * count]
                inverse[pair] = lax.rsqrt(part * (1.0 / half) + 4.0 * norm_epsilon)
                unit[pair] = total[pair] * inverse[pair]
            if with_query:
                for pair in group:
                    query = q_ref[rows_of(step), lanes[pair]]
                    out_ref[rows_of(step - skip), lanes[pair]] = (query + unit[pair][:MINI]).astype(jnp.bfloat16)
            if not with_key:
                continue
            rows = rows_of(step)
            grads = {}
            for pair in group:
                grads[pair] = e_ref[rows, lanes[pair]] * (unit[pair][-MINI:] - t_ref[rows, lanes[pair]])
            products = [(grads[pair] * unit[pair][-MINI:]).astype(jnp.bfloat16) for pair in group]
            along = dot_nn(jnp.concatenate(products, axis=0), block_ones) * (1.0 / half)
            for at, pair in enumerate(group):
                part = along[at * MINI : (at + 1) * MINI]
                change[pair] = (
                    inverse[pair][-MINI:] * (grads[pair] - unit[pair][-MINI:] * part)
                ).astype(jnp.bfloat16)
            back = {}
            for pair, side in sides:
                back[pair, side] = (dot_nn(change[pair], w2_s[2 * pair + side]) * slope[pair, side]).astype(jnp.bfloat16)
            for pair, side in sides:
                head = 2 * pair + side
                here = slice(side * half, side * half + half)
                w2 = w2_out[head] - dot_nn(change[pair].T[here], doubled[pair, side][-MINI:])
                w2_out[head] = w2
                w2_s[head, here, :] = w2.astype(jnp.bfloat16)
                w1 = w1_out[head] - dot_nn(k_ref[rows, lanes[pair]].T[here], back[pair, side])
                w1_out[head] = w1
                w1_s[head, here, :] = w1.astype(jnp.bfloat16)

    if first:
        one(0, False, True)
    lax.fori_loop(skip, steps, lambda step, carry: (one(step, True, True), carry)[1], 0)
    if last:
        one(steps, True, False)
    held_out[...] = q_ref[tokens:]


def run_chunk(shards, rates, weight, row_blocks, w1, w2, held, half, first, last, after=()):
    tokens, depth = shards[0].shape
    heads, _, hidden = w1.shape
    inputs = len(shards)
    count = weight.shape[0] // depth
    state = jax.ShapeDtypeStruct(w1.shape, jnp.float32)
    inside = pl.BlockSpec(memory_space=pltpu.VMEM)
    wide = pltpu.VMEM((tokens, heads * half), jnp.float32)
    return pl.pallas_call(
        functools.partial(chunk_kernel, inputs=inputs, shards=count, half=half, extra=len(after), first=first, last=last),
        in_specs=[pl.BlockSpec(memory_space=pltpu.SMEM)]
        + [inside] * (inputs + 5)
        + [pl.BlockSpec(memory_space=pl.ANY)] * len(after),
        out_specs=[inside] * 4,
        out_shape=[
            jax.ShapeDtypeStruct((tokens + MINI * (last - first), heads * half), jnp.bfloat16),
            state,
            state,
            jax.ShapeDtypeStruct((MINI, heads * half), jnp.float32),
        ],
        scratch_shapes=[
            pltpu.VMEM((tokens, count * depth), jnp.bfloat16),
            pltpu.VMEM((tokens + MINI, heads * half), jnp.float32),
            pltpu.VMEM((tokens, heads * half), jnp.bfloat16),
            wide,
            wide,
            pltpu.VMEM((heads, 2 * half, hidden), jnp.bfloat16),
            pltpu.VMEM((heads, 2 * half, hidden), jnp.bfloat16),
        ],
        compiler_params=pltpu.CompilerParams(vmem_limit_bytes=CHUNK_VMEM),
        name="fast_weights",
    )(row_blocks, *shards, rates, weight, w1, w2, held, *after)


def normalize(values):
    center = values - jnp.mean(values, axis=-1, keepdims=True)
    spread = jnp.mean(center * center, axis=-1, keepdims=True)
    return center * lax.rsqrt(spread + norm_epsilon)


def fast_mlp(inputs, fast_weights):
    hidden = jax.nn.gelu(
        jnp.einsum("bmd,bdf->bmf", inputs, fast_weights[:, 0], precision=highest_precision),
        approximate=True,
    )
    return normalize(
        jnp.einsum("bmf,bdf->bmd", hidden, fast_weights[:, 1], precision=highest_precision)
    )


def minibatch(fast_weights, batch_items):
    queries, key_rows, value_rows, step_rates = batch_items
    target = value_rows - key_rows

    def loss_value(weights_now):
        error = fast_mlp(key_rows, weights_now) - target
        return 0.5 * jnp.sum(step_rates[:, :, None] * error * error) / step_rates.shape[-1]

    gradient = jax.grad(loss_value)(fast_weights)
    fast_weights = fast_weights - gradient
    return (fast_weights, queries + fast_mlp(queries, fast_weights))


def run_items(fast_weights, picked, step_rates):
    batch = picked.shape[0]
    seg_len = picked.shape[2]
    head_dim = picked.shape[3]
    block_count = seg_len // MINI

    def to_blocks(array):
        return array.reshape(batch, block_count, MINI, head_dim).transpose(1, 0, 2, 3)

    rate_blocks = step_rates.reshape(batch, block_count, MINI).transpose(1, 0, 2)
    fast_weights, outputs = lax.scan(
        minibatch,
        fast_weights,
        (to_blocks(picked[:, 0]), to_blocks(picked[:, 1]), to_blocks(picked[:, 2]), rate_blocks),
    )
    return (fast_weights, outputs.transpose(1, 0, 2, 3).reshape(batch, seg_len, head_dim))


def any_size(attn_query, attn_key, attn_value, prompt_len, ttt_weight, init_w1, init_w2t, step_rate):
    videos = attn_query.shape[0]
    seg_len = attn_query.shape[1]
    heads_dev = init_w1.shape[0]
    head_dim = init_w1.shape[1]
    position = lax.broadcasted_iota(jnp.int32, (videos, seg_len), 1)
    usable = (position >= TEXT_SLOTS) | (position < prompt_len)
    queries = attn_query.reshape(videos, seg_len, heads_dev, head_dim)
    key_rows = attn_key.reshape(videos, seg_len, heads_dev, head_dim)
    value_rows = attn_value.reshape(videos, seg_len, heads_dev, head_dim)
    scores = jnp.einsum(
        "vqhd,vkhd->vhqk", queries, key_rows, preferred_element_type=jnp.float32
    ) * head_dim ** (-0.5)
    scores = jnp.where(usable[:, None, None, :], scores, -1e30)
    largest = jnp.max(scores, axis=-1, keepdims=True)
    exponent = jnp.exp(scores - largest)
    weights = (exponent / jnp.sum(exponent, axis=-1, keepdims=True)).astype(jnp.bfloat16)
    attended = jnp.einsum(
        "vhqk,vkhd->vqhd", weights, value_rows, preferred_element_type=jnp.float32
    )
    attended = attended.astype(jnp.bfloat16).reshape(videos, seg_len, heads_dev * head_dim)
    features = lax.all_gather(attended, "head", axis=2, tiled=True)
    feature_full = features.astype(jnp.float32)
    normed = (
        feature_full
        * lax.rsqrt(jnp.mean(feature_full * feature_full, axis=-1, keepdims=True) + rms_epsilon)
    ).astype(jnp.bfloat16)
    projected = jnp.dot(
        normed.reshape(videos * seg_len, normed.shape[2]),
        ttt_weight,
        preferred_element_type=jnp.float32,
    )
    projected = projected.reshape(videos, seg_len, heads_dev, 3, head_dim).transpose(0, 2, 3, 1, 4)
    step_rates = step_rate * usable[:, None, :].astype(jnp.float32)
    init_stack = jnp.stack([init_w1, init_w2t], axis=1)
    seg_count = lax.axis_size("seg")
    item_count = videos * heads_dev
    per_device = (item_count + seg_count - 1) // seg_count
    padded = per_device * seg_count
    item_inputs = projected.reshape(item_count, 3, seg_len, head_dim)
    item_inputs = jnp.pad(item_inputs, ((0, padded - item_count), (0, 0), (0, 0), (0, 0)))
    item_rates = step_rates.reshape(item_count, 1, seg_len, 1)
    item_rates = jnp.pad(item_rates, ((0, padded - item_count), (0, 0), (0, 0), (0, 0)))
    sequences, rate_rows = (
        lax.all_to_all(
            item_inputs.astype(jnp.bfloat16), "seg", split_axis=0, concat_axis=2, tiled=True
        ).astype(item_inputs.dtype),
        lax.all_to_all(
            item_rates.astype(jnp.bfloat16), "seg", split_axis=0, concat_axis=2, tiled=True
        ).astype(item_rates.dtype),
    )
    item_global = lax.axis_index("seg") * per_device + jnp.arange(per_device, dtype=jnp.int32)
    head_of = item_global % heads_dev
    start = jnp.take(init_stack, head_of, axis=0)
    final_weights, outputs = run_items(
        start, sequences, rate_rows.reshape(per_device, sequences.shape[2])
    )
    returned = lax.all_to_all(
        outputs.astype(jnp.bfloat16), "seg", split_axis=1, concat_axis=0, tiled=True
    ).astype(outputs.dtype)
    results = returned[:item_count].reshape(videos, heads_dev, seg_len, head_dim)
    results = results.transpose(0, 2, 1, 3).reshape(videos, seg_len, heads_dev * head_dim)
    return results.astype(jnp.bfloat16)


def take_kernel(*refs, at, rows):
    out = refs[-1]
    out[:rows] = refs[0][at : at + rows, : out.shape[1]]
    if out.shape[0] > rows:
        out[rows:] = refs[1][...]


def take(source, at, rows, columns, second=None, after=(), beside=()):
    inputs = [source] if second is None else [source, second]
    return pl.pallas_call(
        functools.partial(take_kernel, at=at, rows=rows),
        in_specs=[pl.BlockSpec(memory_space=pltpu.VMEM)] * len(inputs)
        + [pl.BlockSpec(memory_space=pltpu.VMEM)] * len(beside)
        + [pl.BlockSpec(memory_space=pl.ANY)] * len(after),
        out_specs=pl.BlockSpec(memory_space=pltpu.VMEM),
        out_shape=jax.ShapeDtypeStruct((rows * len(inputs), columns), source.dtype),
        cost_estimate=pl.CostEstimate(flops=1, transcendentals=0, bytes_accessed=1),
        compiler_params=pltpu.CompilerParams(vmem_limit_bytes=8 * 1024 * 1024),
        name="take",
    )(*inputs, *beside, *after)


CHUNK_PARTS = (4, 4, 4, 2, 2)
LAG = 2
AHEAD = 2
WAT = 2


def chunk_sizes(tokens):
    if tokens % (16 * MINI):
        return [tokens]
    return [part * (tokens // 16) for part in CHUNK_PARTS]


NEAR = [(0, 1), (1, 0), (2, 3), (3, 2)]
FAR = [(0, 2), (2, 0), (1, 3), (3, 1)]


def by_video(attn_query, attn_key, attn_value, prompt_len, ttt_weight, init_w1, init_w2t, step_rate):
    videos, seg_len, channels = attn_query.shape
    half = init_w1.shape[1]
    segments = lax.axis_size("seg")
    mixed = attention(attn_query, attn_key, attn_value, prompt_len[:, 0], step_rate, half)
    mine = lax.all_to_all(mixed, "seg", split_axis=0, concat_axis=0, tiled=True)
    mine = mine.reshape(segments * seg_len, mixed.shape[2])
    rates = mine[:, channels:]
    w1 = init_w1
    held = jnp.zeros((MINI, channels), jnp.float32)
    w2 = init_w2t - jnp.mean(init_w2t, axis=1, keepdims=True)
    tokens = segments * seg_len
    chunk = tokens // 4
    count = lax.axis_size("head")
    me = lax.axis_index("head")
    row_blocks = me ^ jnp.array([0, 2, 1, 3], jnp.int32)
    sizes = chunk_sizes(tokens)
    ends = [sum(sizes[: c + 1]) for c in range(len(sizes))]
    chunks = len(sizes)
    outs, own, far, near = [], [], [], []

    def send_far(c, after):
        own.append(take(mine, ends[c] - sizes[c], sizes[c], channels, after=after, beside=[ttt_weight] if c == WAT else []))
        far.append(lax.ppermute(own[c], "head", FAR))

    def send_near(c, after):
        both = take(own[c], 0, sizes[c], channels, far[c], after)
        near.append(lax.ppermute(both, "head", NEAR))
        return both

    for c in range(min(AHEAD, chunks)):
        send_far(c, [])
    for c in range(chunks + 1):
        if c < chunks:
            both = send_near(c, [outs[c - LAG]] if c >= LAG else [])
        if c + AHEAD < chunks:
            send_far(c + AHEAD, [both])
        if c > 0:
            d = c - 1
            after = [own[c + AHEAD]] if c + AHEAD < chunks else [both] if c < chunks else []
            rate = rates[ends[d] - sizes[d] : ends[d]]
            out, w1, w2, held = run_chunk(
                [own[d], far[d], near[d]], rate, ttt_weight, row_blocks, w1, w2, held, half, d == 0, d + 1 == chunks, after
            )
            outs.append(out)
    result = jnp.concatenate(outs, axis=0).reshape(videos, seg_len, channels)
    return lax.all_to_all(result, "seg", split_axis=0, concat_axis=0, tiled=True)


def body(attn_query, attn_key, attn_value, prompt_len, ttt_weight, init_w1, init_w2t, step_rate):
    videos, seg_len, channels = attn_query.shape
    heads, half, hidden = init_w1.shape
    whole_pairs = heads % 2 == 0 and 2 * half == 128 and hidden % 128 == 0
    fits = seg_len % 128 == 0 and heads <= 128
    run = by_video if videos == lax.axis_size("seg") and whole_pairs and fits and lax.axis_size("head") == 4 else any_size
    return run(attn_query, attn_key, attn_value, prompt_len, ttt_weight, init_w1, init_w2t, step_rate)


def solution(mesh):
    return jax.shard_map(
        body,
        mesh=mesh,
        in_specs=(
            P(None, "seg", "head"),
            P(None, "seg", "head"),
            P(None, "seg", "head"),
            P(None, "seg"),
            P(None, "head"),
            P("head", None, None),
            P("head", None, None),
            P(None, "head", "seg"),
        ),
        out_specs=P(None, "seg", "head"),
        check_vma=False,
    )
```
